32 devices in a mesh: gx: 4 (over z), gy: 2 (over y), gz: 4 (over x, core).
Axes of the slice: x: 2, y: 2, z: 4, core: 2. Of those that a mesh axis runs over, the one named last changes fastest.
Arguments:
- right_side: float32 [4, 2, 4, 6, 1024], P('gx', 'gy', 'gz'), may hold values from -18 to 18
- grain_diag: float32 [4, 2, 4, 6, 1024], P('gx', 'gy', 'gz'), may hold values from 0.05 to 0.5
- stiffness: float32 [4, 4], replicated, may hold values from 0.3 to 3
- contact_own: int32 [4, 2, 4, 3072], P('gx', 'gy', 'gz'), may hold values from 0 to 1023, as said below
- contact_slot: int32 [4, 2, 4, 3072], P('gx', 'gy', 'gz'), may hold values from 0 to 7679, as said below
- contact_type: int32 [4, 2, 4, 3072], P('gx', 'gy', 'gz'), may hold values from 0 to 4, as said below
- contact_normal: float32 [4, 2, 4, 3, 3072], P('gx', 'gy', 'gz'), may hold values from -1 to 1, as said below
- contact_radii: float32 [4, 2, 4, 2, 3072], P('gx', 'gy', 'gz'), may hold values from 0.4 to 1
Outputs:
- solution_field: float32 [4, 2, 4, 6, 1024], P('gx', 'gy', 'gz')
- residual: float32 [4, 2, 4, 6, 1024], P('gx', 'gy', 'gz')
The draws below stay inside these ranges and needn't reach their ends.
Inputs may be any that keep to these rules, and one draw needn't show every extreme that they name: `contact_normal`: each normal has unit length. `contact_own`: in the first 2240 slots of a block the own grain differs from the partner; in the last 832 slots the own grain is one of the block's first 256 grains. `contact_slot`: the first 2240 slots of a block hold values below 1024; the slots 3072 - 832 + k * 32 to 2240 + (k + 1) * 32 - 1, for k = 0 to 25, hold values from 1024 + k * 256 to 1024 + (k + 1) * 256 - 1. `contact_type`: the value 4 marks an empty slot.
All inputs are finite; a program needn't handle non-finite values.
Results may differ from the reference program's by a relative error of at most 0.00018.
Values sent between devices are 32-bit elements; how exact they have to be, the bound alone decides.
No kernel may reach another device: no remote copies, remote signals or barrier semaphores. Data moves between devices by JAX's collectives and lax.ppermute only.
A program may use at most 64 MiB of HBM per device.

```python
import math
import jax
import jax.numpy as jnp

GRAINS = 1024
RIM = 256
CONTACTS = 3072
GROUP = 32
REMOTE = 832
TYPES = 4
ITERS = 4
BX = 4
BY = 2
BZ = 4


def contact_tables(key):
    base = jax.random.fold_in(key, 7301)
    keys = jax.random.split(base, 6)
    lead = (BX, BY, BZ)
    local_count = CONTACTS - REMOTE
    own_near = jax.random.randint(keys[0], lead + (local_count,), 0, GRAINS, dtype=jnp.int32)
    offset = jax.random.randint(keys[1], lead + (local_count,), 1, GRAINS, dtype=jnp.int32)
    slot_near = (own_near + offset) % GRAINS
    own_far = jax.random.randint(keys[2], lead + (REMOTE,), 0, RIM, dtype=jnp.int32)
    neighbour = jnp.broadcast_to(jnp.arange(REMOTE, dtype=jnp.int32) // GROUP, lead + (REMOTE,))
    ghost = jax.random.randint(keys[4], lead + (REMOTE,), 0, RIM, dtype=jnp.int32)
    slot_far = GRAINS + neighbour * RIM + ghost
    ctype = jax.random.randint(keys[5], lead + (CONTACTS,), 0, TYPES + 1, dtype=jnp.int32)
    owners = jnp.concatenate([own_near, own_far], axis=-1)
    slots = jnp.concatenate([slot_near, slot_far], axis=-1)
    return (owners, slots, ctype)


def draw_contact_own(key, part):
    return contact_tables(key)[0]


def draw_contact_slot(key, part):
    return contact_tables(key)[1]


def draw_contact_type(key, part):
    return contact_tables(key)[2]


def draw_contact_normal(key, part):
    inner = jax.random.fold_in(key, 4409)
    vectors = jax.random.normal(inner, (BX, BY, BZ, 3, CONTACTS), jnp.float32)
    length = jnp.sqrt(jnp.sum(vectors * vectors, axis=3, keepdims=True) + 1e-12)
    return vectors / length


def draw_right_side(key, part):
    inner = jax.random.fold_in(key, 1187)
    index = (jnp.arange(BX)[:, None, None] * BY + jnp.arange(BY)[None, :, None]) * BZ + jnp.arange(BZ)[None, None, :]
    ramp = index.astype(jnp.float32) / max(BX * BY * BZ - 1, 1)
    scale = (1.0 + 2.0 * ramp)[:, :, :, None, None]
    values = jnp.clip(jax.random.normal(inner, (BX, BY, BZ, 6, GRAINS), jnp.float32), -6.0, 6.0) * scale
    return values


def level_of(stream_key, extent, shards, low, top_value):
    def one(position, shards_of):
        heights = jax.random.uniform(jax.random.fold_in(jax.random.fold_in(stream_key, 6), position), (shards_of,), jnp.float32, low / len(shards), top_value / len(shards))
        return jnp.repeat(jnp.exp(heights), extent[position] // shards_of).reshape((-1,) + (1,) * (len(extent) - position - 1))

    loudness = one(*shards[0])
    for cut in shards[1:]:
        loudness = loudness * one(*cut)
    return loudness


def setup_inputs(seed: int = 0) -> dict:
    seeds = jax.random.split(jax.random.key(seed), 9)
    return {
        "right_side": draw_right_side(jax.random.fold_in(seeds[8], 71), 0),
        "grain_diag": jnp.clip(jnp.exp(math.log(0.5) - 2.3025851 * jax.random.uniform(seeds[1], (BX, BY, BZ, 6, GRAINS), jnp.float32) ** level_of(seeds[1], (BX, BY, BZ, 6, GRAINS), ((0, 4), (1, 2), (2, 4)), -0.2, 0.2)), 0.05, 0.5),
        "stiffness": jnp.clip(jnp.exp(jax.random.uniform(seeds[2], (4, TYPES), jnp.float32, math.log(0.3), math.log(3.0))), 0.3, 3.0),
        "contact_own": draw_contact_own(jax.random.fold_in(seeds[8], 71), 0),
        "contact_slot": draw_contact_slot(jax.random.fold_in(seeds[8], 71), 0),
        "contact_type": draw_contact_type(jax.random.fold_in(seeds[8], 71), 0),
        "contact_normal": draw_contact_normal(jax.random.fold_in(seeds[8], 71), 0),
        "contact_radii": jnp.clip(jnp.exp(math.log(1.0) - 0.9162907 * jax.random.uniform(seeds[7], (BX, BY, BZ, 2, CONTACTS), jnp.float32) ** level_of(seeds[7], (BX, BY, BZ, 2, CONTACTS), ((0, 4), (1, 2), (2, 4)), -0.2, 0.2)), 0.4, 1.0),
    }


def cross(left, right):
    return jnp.stack([left[1] * right[2] - left[2] * right[1],
                      left[2] * right[0] - left[0] * right[2],
                      left[0] * right[1] - left[1] * right[0]])


def lookup(stiffness, ctype):
    total = jnp.zeros((4,) + ctype.shape, stiffness.dtype)
    for which in range(stiffness.shape[1]):
        total = total + stiffness[:, which:which + 1] * (ctype == which)[None].astype(stiffness.dtype)
    return total


def contact_response(first_u, second_u, normal, radii, coeff):
    normal_k, shear_k, roll_k, twist_k = coeff[0], coeff[1], coeff[2], coeff[3]
    first_r, second_r = radii[0], radii[1]
    delta = second_u[:3] - second_r * cross(second_u[3:], normal) - first_u[:3] - first_r * cross(first_u[3:], normal)
    along = jnp.sum(normal * delta, axis=0)
    force = shear_k * delta + (normal_k - shear_k) * along * normal
    theta = second_u[3:] - first_u[3:]
    twist = jnp.sum(normal * theta, axis=0)
    moment = roll_k * theta + (twist_k - roll_k) * twist * normal
    lever = cross(normal, force)
    on_first = jnp.concatenate([force, first_r * lever + moment], axis=0)
    on_second = jnp.concatenate([-force, second_r * lever - moment], axis=0)
    return on_first, on_second


def flatten_field(array):
    return jnp.moveaxis(array, 3, 0).reshape(array.shape[3], -1)


def reference(right_side, grain_diag, stiffness, contact_own, contact_slot, contact_type, contact_normal, contact_radii):
    rhs = flatten_field(right_side)
    diag = flatten_field(grain_diag)
    normal = flatten_field(contact_normal)
    radii = flatten_field(contact_radii)
    block_x = jnp.arange(BX, dtype=jnp.int32)[:, None, None, None]
    block_y = jnp.arange(BY, dtype=jnp.int32)[None, :, None, None]
    block_z = jnp.arange(BZ, dtype=jnp.int32)[None, None, :, None]
    base = ((block_x * BY + block_y) * BZ + block_z) * GRAINS
    remote = contact_slot >= GRAINS
    rel = jnp.maximum(contact_slot - GRAINS, 0)
    kk = rel // RIM
    full = kk + (kk >= 13).astype(jnp.int32)
    off_x = full // 9 - 1
    off_y = (full // 3) % 3 - 1
    off_z = full % 3 - 1
    other = ((((block_x + off_x) % BX) * BY + (block_y + off_y) % BY) * BZ + (block_z + off_z) % BZ) * GRAINS
    first = (base + contact_own).reshape(-1).astype(jnp.int32)
    second = jnp.where(remote, other + rel % RIM, base + contact_slot).reshape(-1).astype(jnp.int32)
    coeff = lookup(stiffness, contact_type.reshape(-1))

    def operate(field):
        on_first, on_second = contact_response(field[:, first], field[:, second], normal, radii, coeff)
        forces = jnp.zeros_like(field).at[:, first].add(on_first).at[:, second].add(on_second)
        return diag * field - forces

    solution_field = jnp.zeros_like(rhs)
    residual = rhs
    direction = rhs
    norm_now = jnp.sum(residual * residual)
    for step in range(ITERS):
        image = operate(direction)
        alpha = norm_now / jnp.sum(direction * image)
        solution_field = solution_field + alpha * direction
        residual = residual - alpha * image
        norm_next = jnp.sum(residual * residual)
        direction = residual + (norm_next / norm_now) * direction
        norm_now = norm_next

    def unflatten(field):
        return jnp.moveaxis(field.reshape(6, BX, BY, BZ, GRAINS), 0, 3)

    return unflatten(solution_field), unflatten(residual)
```

```python
import functools

import jax
import jax.numpy as jnp
from jax import lax
from jax.experimental import pallas as pl
from jax.experimental.pallas import tpu as pltpu
from jax.sharding import PartitionSpec as P

ITERS = 4
AXES = ("gx", "gy", "gz")
LANES = 128
FIELDS = 6


class Plan:
    def __init__(self, mesh, grains, contacts, types):
        self.counts = tuple(mesh.shape[axis] for axis in AXES)
        self.devices = self.counts[0] * self.counts[1] * self.counts[2]
        self.grains = grains
        self.rim = grains // 4
        self.group = grains // 32
        self.contacts = contacts
        self.types = types
        self.near = contacts - 26 * self.group
        self.near_tiles = -(-self.near // LANES)
        self.tiles = contacts // LANES
        self.grain_tiles = grains // LANES
        self.rim_tiles = self.rim // LANES
        sides = {}
        for k in range(26):
            whole = k + (1 if k >= 13 else 0)
            offset = (whole // 9 - 1, whole // 3 % 3 - 1, whole % 3 - 1)
            delta = tuple(o % c for o, c in zip(offset, self.counts))
            sides.setdefault(delta, []).append(k)
        self.sides = sorted(sides.items())
        self.far = len(self.sides)
        most = max(len(groups) for groups in sides.values())
        self.half = -(-most * self.group // (LANES // 2)) * (LANES // 2)
        assert self.half * 2 == LANES

    def neighbours(self):
        place = [lax.axis_index(axis) for axis in AXES]
        found = []
        for delta, _ in self.sides:
            x, y, z = (lax.rem(p + d, c) for p, d, c in zip(place, delta, self.counts))
            found.append((x * self.counts[1] + y) * self.counts[2] + z)
        return found


def row_of(ref, row, stride, count):
    return ref[pl.ds(row, count, stride=stride), :]


def lane_gather(tiles, index):
    low = jnp.bitwise_and(index, LANES - 1)
    high = lax.shift_right_logical(index, 7)
    total = jnp.zeros(tiles[0].shape, tiles[0].dtype)
    for which, tile in enumerate(tiles):
        found = jnp.take_along_axis(tile, low, axis=1, mode="promise_in_bounds")
        total = jnp.where(high == which, found, total)
    return total


def spread(ref, row):
    return jnp.broadcast_to(ref[row : row + 1, :], (8, LANES))


def coefficients(stiff_ref, kind, types, valid=None):
    found = []
    for which in range(4):
        total = jnp.zeros(kind.shape, jnp.float32)
        for t in range(types):
            total = jnp.where(kind == t, stiff_ref[which, t], total)
        if valid is not None:
            total = jnp.where(valid, total, 0.0)
        found.append(total)
    normal_k, shear_k, roll_k, twist_k = found
    return shear_k, normal_k - shear_k, roll_k, twist_k - roll_k


def response(first, second, table):
    n = table[0:3]
    first_r, second_r, shear_k, normal_d, roll_k, twist_d = table[3:]
    p = [second_r * second[3 + c] + first_r * first[3 + c] for c in range(3)]
    delta = []
    for c in range(3):
        a, b = (c + 1) % 3, (c + 2) % 3
        delta.append(second[c] - first[c] - (p[a] * n[b] - p[b] * n[a]))
    theta = [second[3 + c] - first[3 + c] for c in range(3)]
    along = normal_d * (n[0] * delta[0] + n[1] * delta[1] + n[2] * delta[2])
    twist = twist_d * (n[0] * theta[0] + n[1] * theta[1] + n[2] * theta[2])
    force = [shear_k * delta[c] + along * n[c] for c in range(3)]
    moment = [roll_k * theta[c] + twist * n[c] for c in range(3)]
    lever = []
    for c in range(3):
        a, b = (c + 1) % 3, (c + 2) % 3
        lever.append(n[a] * force[b] - n[b] * force[a])
    return force, lever, moment


def two_parts(value):
    high = value.astype(jnp.bfloat16)
    low = (value - high.astype(jnp.float32)).astype(jnp.bfloat16)
    return jnp.concatenate([high, low], axis=0)


def one_hot(index_tile, width):
    rows = index_tile.shape[0]
    padded = index_tile
    if rows < LANES:
        padded = jnp.concatenate(
            [index_tile, jnp.zeros((LANES - rows, LANES), index_tile.dtype)], axis=0
        )
    turned = jnp.transpose(padded)
    lane = lax.broadcasted_iota(jnp.int32, (LANES, width), 1).astype(jnp.float32)

    def make(row):
        return jnp.where(turned[:, row : row + 1] == lane, 1.0, 0.0).astype(jnp.bfloat16)

    return make


def send_setup(plan, own, slot, kind, normal, radii, rhs, message, mine, stack):
    first = plan.near // LANES
    for t in range(first, plan.tiles):
        at = (t - first) * 8
        lanes = slice(t * LANES, (t + 1) * LANES)
        stack[at : at + 1, :] = own[t : t + 1, :].astype(jnp.float32)
        stack[at + 1 : at + 2, :] = jnp.bitwise_and(slot[t : t + 1, :], plan.rim - 1).astype(
            jnp.float32
        )
        stack[at + 2 : at + 3, :] = kind[t : t + 1, :].astype(jnp.float32)
        stack[at + 3 : at + 6, :] = normal[:, lanes]
        stack[at + 6 : at + 8, :] = radii[:, lanes]
    lane = lax.broadcasted_iota(jnp.int32, (8, LANES), 1)
    row = lax.broadcasted_iota(jnp.int32, (8, LANES), 0)
    where = plan.neighbours()
    for e, (_, groups) in enumerate(plan.sides):
        chunk = jnp.where(row == 2, float(plan.types), 0.0)
        for j, k in enumerate(groups):
            place = plan.near + k * plan.group
            t, inside = place // LANES, place % LANES
            tile = stack[(t - first) * 8 : (t - first) * 8 + 8, :]
            turn = (j * plan.group - inside) % LANES
            if turn:
                tile = pltpu.roll(tile, turn, 1)
            here = (lane >= j * plan.group) & (lane < (j + 1) * plan.group)
            chunk = jnp.where(here, tile, chunk)
        mine[e * 8 : e * 8 + 8, :] = chunk
        message[where[e], 0:8, :] = chunk
        for t in range(plan.rim_tiles):
            message[where[e], 8 + 8 * t : 8 + 8 * t + FIELDS, :] = rhs[
                :, t * LANES : (t + 1) * LANES
            ]


def near_part(plan, field, diag, own, slot, table, hot, image, seen, push, left):
    rows = plan.near_tiles
    tiles = [field[:, s * LANES : (s + 1) * LANES] for s in range(plan.grain_tiles)]
    for side, index in enumerate((own, slot)):
        for t in range(rows):
            at = (side * rows + t) * 8
            seen[at : at + 8, :] = lane_gather(tiles, spread(index, t))
    first = [row_of(seen, c, 8, rows) for c in range(FIELDS)]
    second = [row_of(seen, rows * 8 + c, 8, rows) for c in range(FIELDS)]
    consts = [table[k, 0:rows, :] for k in range(9)]
    force, lever, moment = response(first, second, consts)
    for c in range(3):
        push[pl.ds(c, rows, stride=8), :] = force[c]
        push[pl.ds(3 + c, rows, stride=8), :] = consts[3] * lever[c] + moment[c]
        push[pl.ds(rows * 8 + c, rows, stride=8), :] = -force[c]
        push[pl.ds(rows * 8 + 3 + c, rows, stride=8), :] = consts[4] * lever[c] - moment[c]
    zero = jnp.zeros((2 * rows, LANES), jnp.float32)
    for c in range(FIELDS, 8):
        push[pl.ds(c, 2 * rows, stride=8), :] = zero
    parts = plan.grains // plan.rim
    for side, index in enumerate((own, slot)):
        for t in range(rows):
            at = side * rows + t
            value = push[at * 8 : at * 8 + 8, :]
            part = lax.div(spread(index, t), plan.rim)
            for q in range(parts):
                left[q * 16 : q * 16 + 16, at * LANES : (at + 1) * LANES] = two_parts(
                    jnp.where(part == q, value, 0.0)
                )
    total = jnp.dot(left[...], hot[...], preferred_element_type=jnp.float32)
    for q in range(parts):
        lanes = slice(q * plan.rim, (q + 1) * plan.rim)
        force = total[q * 16 : q * 16 + 8, :] + total[q * 16 + 8 : q * 16 + 16, :]
        image[:, lanes] = diag[:, lanes] * field[:, lanes] - force


def near_first(
    plan, stiff, own, slot, kind, normal, radii, rhs, diag6,
    image, table, hot, field, diag, seen, push, left,
):
    rows = plan.near_tiles
    field[...] = jnp.zeros(field.shape, jnp.float32)
    diag[...] = jnp.zeros(diag.shape, jnp.float32)
    field[0:FIELDS, :] = rhs[...]
    diag[0:FIELDS, :] = diag6[...]
    for t in range(rows):
        lanes = slice(t * LANES, (t + 1) * LANES)
        for c in range(3):
            table[c, t : t + 1, :] = normal[c : c + 1, lanes]
        for c in range(2):
            table[3 + c, t : t + 1, :] = radii[c : c + 1, lanes]
    lane = lax.broadcasted_iota(jnp.int32, (rows, LANES), 1)
    line = lax.broadcasted_iota(jnp.int32, (rows, LANES), 0)
    valid = line * LANES + lane < plan.near
    for k, value in enumerate(coefficients(stiff, kind[0:rows, :], plan.types, valid)):
        table[5 + k, 0:rows, :] = value
    for side, index in enumerate((own, slot)):
        low = jnp.bitwise_and(index[...], plan.rim - 1).astype(jnp.float32)
        make = one_hot(low, plan.rim)
        for t in range(rows):
            at = (side * rows + t) * LANES
            hot[at : at + LANES, :] = make(t)
    near_part(plan, field, diag, own, slot, table, hot, image, seen, push, left)


def far_forces(plan, local, there, table, hot, push, left):
    rows = plan.far
    first = [row_of(local, c, 8, rows) for c in range(FIELDS)]
    second = [row_of(there, c, 8, rows) for c in range(FIELDS)]
    consts = [table[k, 0:rows, :] for k in range(9)]
    force, lever, moment = response(first, second, consts)
    for c in range(3):
        push[pl.ds(c, rows, stride=8), :] = force[c]
        push[pl.ds(3 + c, rows, stride=8), :] = consts[3] * lever[c] + moment[c]
    zero = jnp.zeros((rows, LANES), jnp.float32)
    for c in range(FIELDS, 8):
        push[pl.ds(c, rows, stride=8), :] = zero
    for e in range(rows):
        left[:, e * LANES : (e + 1) * LANES] = two_parts(push[e * 8 : e * 8 + 8, :])
    total = jnp.dot(left[...], hot[...], preferred_element_type=jnp.float32)
    return total[0:8, :] + total[8:16, :]


def send_rim(plan, field, index, sums, message, local):
    row = lax.broadcasted_iota(jnp.int32, (8, LANES), 0)
    base = jnp.where(row == FIELDS, sums[0], jnp.where(row == FIELDS + 1, sums[1], 0.0))
    message[...] = jnp.broadcast_to(base[None], message.shape)
    tiles = [field[:, t * LANES : (t + 1) * LANES] for t in range(plan.rim_tiles)]
    where = plan.neighbours()
    for e in range(plan.far):
        tile = lane_gather(tiles, spread(index, e))
        local[e * 8 : e * 8 + 8, :] = tile
        message[where[e], :, :] = jnp.where(row < FIELDS, pltpu.roll(tile, plan.half, 1), base)


def partial_sum(left, right):
    product = left * right
    total = product[:, 0:LANES]
    for t in range(1, product.shape[1] // LANES):
        total = total + product[:, t * LANES : (t + 1) * LANES]
    return jnp.sum(total, axis=0, keepdims=True)


def full_sum(received, row):
    return jnp.sum(jnp.sum(received[:, row, :], axis=0, keepdims=True), axis=1, keepdims=True)


def far_first(
    plan, stiff, received, mine, field, image,
    w, message, table, index, hot, local, merged, there, push, left,
):
    lane8 = lax.broadcasted_iota(jnp.int32, (8, LANES), 1)
    where = plan.neighbours()
    rows = plan.far
    for e in range(rows):
        own = pltpu.roll(mine[e * 8 : e * 8 + 8, :], plan.half, 1)
        merged[e * 8 : e * 8 + 8, :] = jnp.where(
            lane8 < plan.half, received[where[e], 0:8, :], own
        )
    mirror = lax.broadcasted_iota(jnp.int32, (rows, LANES), 1) < plan.half
    row = [row_of(merged, r, 8, rows) for r in range(8)]
    for c in range(3):
        table[c, 0:rows, :] = jnp.where(mirror, -row[3 + c], row[3 + c])
    table[3, 0:rows, :] = jnp.where(mirror, row[7], row[6])
    table[4, 0:rows, :] = jnp.where(mirror, row[6], row[7])
    for k, value in enumerate(coefficients(stiff, row[2], plan.types)):
        table[5 + k, 0:rows, :] = value
    here = jnp.where(mirror, row[1], row[0])
    away = jnp.where(mirror, row[0], row[1]).astype(jnp.int32)
    index[0:rows, :] = here.astype(jnp.int32)
    make = one_hot(here, plan.rim)
    tiles = [field[:, t * LANES : (t + 1) * LANES] for t in range(plan.rim_tiles)]
    for e in range(rows):
        hot[e * LANES : (e + 1) * LANES, :] = make(e)
        local[e * 8 : e * 8 + 8, :] = lane_gather(tiles, spread(index, e))
        ghosts = [received[where[e], 8 + 8 * t : 16 + 8 * t, :] for t in range(plan.rim_tiles)]
        there[e * 8 : e * 8 + 8, :] = lane_gather(
            ghosts, jnp.broadcast_to(away[e : e + 1, :], (8, LANES))
        )
    force = far_forces(plan, local, there, table, hot, push, left)
    w[...] = image[...]
    w[:, 0 : plan.rim] = image[:, 0 : plan.rim] - force
    r = field[...]
    sums = (partial_sum(r, r), partial_sum(w[...], r))
    send_rim(plan, w, index, sums, message, local)


def far_step(plan, number, *refs):
    refs = list(refs)

    def take(count):
        return [refs.pop(0) for _ in range(count)]

    received, image, table, index, hot, local, r, w = take(8)
    if number:
        p, s, z, x, past = take(5)
    last = number == ITERS - 2
    r_new, p_new, s_new, x_new, w_new, past_new = take(6)
    if not last:
        z_new, message, local_new = take(3)
    else:
        (message,) = take(1)
    there, push, left = take(3)

    where = plan.neighbours()
    for e in range(plan.far):
        there[e * 8 : e * 8 + 8, :] = received[where[e], :, :]
    gamma = full_sum(received, FIELDS)
    delta = full_sum(received, FIELDS + 1)
    force = far_forces(plan, local, there, table, hot, push, left)
    q = jnp.concatenate(
        [image[:, 0 : plan.rim] - force, image[:, plan.rim :]], axis=1
    )
    if number:
        beta = gamma / past[0:1, 0:1]
        alpha = gamma / (delta - beta * gamma / past[1:2, 0:1])
        z_now = q + beta * z[...]
        s_now = w[...] + beta * s[...]
        p_now = r[...] + beta * p[...]
        x_new[...] = x[...] + alpha * p_now
    else:
        alpha = gamma / delta
        z_now = q
        s_now = w[...]
        p_now = r[...]
        x_new[...] = alpha * p_now
    r_now = r[...] - alpha * s_now
    w_now = w[...] - alpha * z_now
    r_new[...] = r_now
    w_new[...] = w_now
    p_new[...] = p_now
    s_new[...] = s_now
    past_new[0:1, :] = jnp.broadcast_to(gamma, (1, LANES))
    past_new[1:2, :] = jnp.broadcast_to(alpha, (1, LANES))
    sums = (partial_sum(r_now, r_now), partial_sum(w_now, r_now))
    if not last:
        z_new[...] = z_now
        send_rim(plan, w_new, index, sums, message, local_new)
    else:
        base = jnp.concatenate(sums, axis=0)
        message[...] = jnp.broadcast_to(base[None], message.shape)


def finish(plan, received, r, w, p, s, x, past, x_out, r_out):
    gamma = full_sum(received, 0)
    delta = full_sum(received, 1)
    beta = gamma / past[0:1, 0:1]
    alpha = gamma / (delta - beta * gamma / past[1:2, 0:1])
    here = slice(0, FIELDS)
    x_out[...] = x[here, :] + alpha * (r[here, :] + beta * p[here, :])
    r_out[...] = r[here, :] - alpha * (w[here, :] + beta * s[here, :])


def shards(
    mesh,
    right_side,
    grain_diag,
    stiffness,
    contact_own,
    contact_slot,
    contact_type,
    contact_normal,
    contact_radii,
):
    rhs = right_side[0, 0, 0]
    diag6 = grain_diag[0, 0, 0]
    plan = Plan(mesh, rhs.shape[1], contact_own.shape[-1], stiffness.shape[1])
    own = contact_own.reshape(plan.tiles, LANES)
    slot = contact_slot.reshape(plan.tiles, LANES)
    kind = contact_type.reshape(plan.tiles, LANES)
    normal = contact_normal[0, 0, 0]
    radii = contact_radii[0, 0, 0]
    f32, bf16, i32 = jnp.float32, jnp.bfloat16, jnp.int32
    vmem = pltpu.MemorySpace.VMEM
    wide = (8, plan.grains)
    far = (plan.far * 8, LANES)
    far_table = (9, -(-plan.far // 8) * 8, LANES)
    near_table = (9, -(-plan.near_tiles // 8) * 8, LANES)
    near_rows = 2 * plan.near_tiles
    parts = plan.grains // plan.rim

    def call(body, outs, scratch, *args, smem=()):
        specs = [
            pl.BlockSpec(memory_space=pltpu.MemorySpace.SMEM if i in smem else vmem)
            for i in range(len(args))
        ]
        return pl.pallas_call(
            functools.partial(body, plan),
            out_shape=outs,
            in_specs=specs,
            out_specs=jax.tree.map(lambda _: pl.BlockSpec(memory_space=vmem), outs),
            scratch_shapes=scratch,
            compiler_params=pltpu.CompilerParams(vmem_limit_bytes=40 * 2**20),
        )(*args)

    def exchange(message):
        return lax.all_to_all(message, AXES, 0, 0)

    def shape(dims, dtype=f32):
        return jax.ShapeDtypeStruct(dims, dtype)

    tile = (plan.devices, 8, LANES)
    near_scratch = [
        vmem((near_rows * 8, LANES), f32),
        vmem((near_rows * 8, LANES), f32),
        vmem((parts * 16, near_rows * LANES), bf16),
    ]
    far_scratch = [vmem(far, f32), vmem(far, f32), vmem((16, plan.far * LANES), bf16)]

    message, mine = call(
        send_setup,
        [shape((plan.devices, 8 + 8 * plan.rim_tiles, LANES)), shape(far)],
        [vmem(((plan.tiles - plan.near // LANES) * 8, LANES), f32)],
        own, slot, kind, normal, radii, rhs,
    )
    received = exchange(message)
    image, near_const, near_hot, field, diag = call(
        near_first,
        [shape(wide), shape(near_table), shape((near_rows * LANES, plan.rim), bf16), shape(wide), shape(wide)],
        near_scratch,
        stiffness, own, slot, kind, normal, radii, rhs, diag6,
        smem=(0,),
    )
    w, message, far_const, index, far_hot, local = call(
        far_first,
        [
            shape(wide),
            shape(tile),
            shape(far_table),
            shape(far_table[1:], i32),
            shape((plan.far * LANES, plan.rim), bf16),
            shape(far),
        ],
        [vmem(far, f32)] + far_scratch,
        stiffness, received, mine, field, image,
        smem=(0,),
    )
    r = field
    state = ()
    for number in range(ITERS - 1):
        received = exchange(message)
        image = call(
            lambda plan, f, d, o, s, t, h, out, *scratch: near_part(
                plan, f, d, o, s, t, h, out, *scratch
            ),
            shape(wide),
            near_scratch,
            w, diag, own, slot, near_const, near_hot,
        )
        last = number == ITERS - 2
        outs = [shape(wide)] * 5 + [shape((8, LANES))]
        if last:
            outs = outs + [shape((plan.devices, 2, LANES))]
        else:
            outs = outs + [shape(wide), shape(tile), shape(far)]
        made = call(
            lambda plan, *refs, number=number: far_step(plan, number, *refs),
            outs,
            far_scratch,
            received, image, far_const, index, far_hot, local, r, w, *state,
        )
        r, p, s, x, w, past = made[:6]
        if last:
            message = made[6]
        else:
            z, message, local = made[6:]
            state = (p, s, z, x, past)
    received = exchange(message)
    out = [shape((FIELDS, plan.grains))] * 2
    solution_field, residual = call(finish, out, [], received, r, w, p, s, x, past)
    return (solution_field[None, None, None], residual[None, None, None])


def solution(mesh):
    vector = P("gx", "gy", "gz", None)
    matrix = P("gx", "gy", "gz", None, None)
    return jax.shard_map(
        functools.partial(shards, mesh),
        mesh=mesh,
        in_specs=(matrix, matrix, P(), vector, vector, vector, matrix, matrix),
        out_specs=(matrix, matrix),
        check_vma=False,
    )
```

```python
import functools

import jax
import jax.numpy as jnp
from jax import lax
from jax.experimental import pallas as pl
from jax.experimental.pallas import tpu as pltpu
from jax.sharding import PartitionSpec as P

ITERS = 4
AXES = ("gx", "gy", "gz")
LANES = 128
FIELDS = 6


class Plan:
    def __init__(self, mesh, grains, contacts, types):
        self.counts = tuple(mesh.shape[axis] for axis in AXES)
        self.devices = self.counts[0] * self.counts[1] * self.counts[2]
        self.grains = grains
        self.rim = grains // 4
        self.group = grains // 32
        self.contacts = contacts
        self.types = types
        self.near = contacts - 26 * self.group
        self.near_tiles = -(-self.near // LANES)
        self.tiles = contacts // LANES
        self.grain_tiles = grains // LANES
        self.rim_tiles = self.rim // LANES
        sides = {}
        for k in range(26):
            whole = k + (1 if k >= 13 else 0)
            offset = (whole // 9 - 1, whole // 3 % 3 - 1, whole % 3 - 1)
            delta = tuple(o % c for o, c in zip(offset, self.counts))
            sides.setdefault(delta, []).append(k)
        self.sides = sorted(sides.items())
        self.far = len(self.sides)
        most = max(len(groups) for groups in sides.values())
        self.half = -(-most * self.group // (LANES // 2)) * (LANES // 2)
        assert self.half * 2 == LANES

    def neighbours(self):
        place = [lax.axis_index(axis) for axis in AXES]
        found = []
        for delta, _ in self.sides:
            x, y, z = (lax.rem(p + d, c) for p, d, c in zip(place, delta, self.counts))
            found.append((x * self.counts[1] + y) * self.counts[2] + z)
        return found


def row_of(ref, row, stride, count):
    return ref[pl.ds(row, count, stride=stride), :]


def lane_gather(tiles, index):
    low = jnp.bitwise_and(index, LANES - 1)
    high = lax.shift_right_logical(index, 7)
    total = jnp.zeros(tiles[0].shape, tiles[0].dtype)
    for which, tile in enumerate(tiles):
        found = jnp.take_along_axis(tile, low, axis=1, mode="promise_in_bounds")
        total = jnp.where(high == which, found, total)
    return total


def spread(ref, row):
    return jnp.broadcast_to(ref[row : row + 1, :], (8, LANES))


def coefficients(stiff_ref, kind, types, valid=None):
    found = []
    for which in range(4):
        total = jnp.zeros(kind.shape, jnp.float32)
        for t in range(types):
            total = jnp.where(kind == t, stiff_ref[which : which + 1, t : t + 1], total)
        if valid is not None:
            total = jnp.where(valid, total, 0.0)
        found.append(total)
    normal_k, shear_k, roll_k, twist_k = found
    return shear_k, normal_k - shear_k, roll_k, twist_k - roll_k


def response(first, second, table):
    n = table[0:3]
    first_r, second_r, shear_k, normal_d, roll_k, twist_d = table[3:]
    p = [second_r * second[3 + c] + first_r * first[3 + c] for c in range(3)]
    delta = []
    for c in range(3):
        a, b = (c + 1) % 3, (c + 2) % 3
        delta.append(second[c] - first[c] - (p[a] * n[b] - p[b] * n[a]))
    theta = [second[3 + c] - first[3 + c] for c in range(3)]
    along = normal_d * (n[0] * delta[0] + n[1] * delta[1] + n[2] * delta[2])
    twist = twist_d * (n[0] * theta[0] + n[1] * theta[1] + n[2] * theta[2])
    force = [shear_k * delta[c] + along * n[c] for c in range(3)]
    moment = [roll_k * theta[c] + twist * n[c] for c in range(3)]
    lever = []
    for c in range(3):
        a, b = (c + 1) % 3, (c + 2) % 3
        lever.append(n[a] * force[b] - n[b] * force[a])
    return force, lever, moment


def three_parts(value):
    high = value.astype(jnp.bfloat16)
    rest = value - high.astype(jnp.float32)
    middle = rest.astype(jnp.bfloat16)
    low = (rest - middle.astype(jnp.float32)).astype(jnp.bfloat16)
    return jnp.concatenate([high, middle], axis=0), low


def fetch(copies, sems):
    started = [
        pltpu.make_async_copy(source, target, sems.at[i])
        for i, (source, target) in enumerate(copies)
    ]
    for copy in started:
        copy.start()
    return started


def one_hot(index_tile, width):
    rows = index_tile.shape[0]
    padded = index_tile
    if rows < LANES:
        padded = jnp.concatenate(
            [index_tile, jnp.zeros((LANES - rows, LANES), index_tile.dtype)], axis=0
        )
    turned = jnp.transpose(padded)
    lane = lax.broadcasted_iota(jnp.int32, (LANES, width), 1).astype(jnp.float32)

    def make(row):
        return jnp.where(turned[:, row : row + 1] == lane, 1.0, 0.0).astype(jnp.bfloat16)

    return make


def send_setup(
    plan, own_h, slot_h, kind_h, normal_h, radii_h, rhs_h,
    message, mine, own, slot, kind, normal, radii, rhs, stack, sems,
):
    first = plan.near // LANES
    lanes = pl.ds(first * LANES, plan.contacts - first * LANES)
    for copy in fetch(
        [
            (own_h, own),
            (slot_h, slot),
            (kind_h, kind),
            (normal_h, normal),
            (radii_h.at[0, 0, 0, :, lanes], radii),
            (rhs_h, rhs),
        ],
        sems,
    ):
        copy.wait()
    for t in range(first, plan.tiles):
        at = (t - first) * 8
        lanes = slice(at * 16, at * 16 + LANES)
        stack[at : at + 1, :] = own[t : t + 1, :].astype(jnp.float32)
        stack[at + 1 : at + 2, :] = jnp.bitwise_and(slot[t : t + 1, :], plan.rim - 1).astype(
            jnp.float32
        )
        stack[at + 2 : at + 3, :] = kind[t : t + 1, :].astype(jnp.float32)
        stack[at + 3 : at + 6, :] = row_of(normal, t, plan.tiles, 3)
        stack[at + 6 : at + 8, :] = radii[:, lanes]
    lane = lax.broadcasted_iota(jnp.int32, (8, LANES), 1)
    row = lax.broadcasted_iota(jnp.int32, (8, LANES), 0)
    where = plan.neighbours()
    ghosts = [row_of(rhs, t, plan.grain_tiles, FIELDS) for t in range(plan.rim_tiles)]
    for e, (_, groups) in enumerate(plan.sides):
        chunk = jnp.where(row == 2, float(plan.types), 0.0)
        for j, k in enumerate(groups):
            place = plan.near + k * plan.group
            t, inside = place // LANES, place % LANES
            tile = stack[(t - first) * 8 : (t - first) * 8 + 8, :]
            turn = (j * plan.group - inside) % LANES
            if turn:
                tile = pltpu.roll(tile, turn, 1)
            here = (lane >= j * plan.group) & (lane < (j + 1) * plan.group)
            chunk = jnp.where(here, tile, chunk)
        mine[e * 8 : e * 8 + 8, :] = chunk
        packed = jnp.where(lane < plan.half, chunk, pltpu.roll(pltpu.roll(chunk, 4, 0), plan.half, 1))
        for t in range(plan.rim_tiles):
            message[where[e], 8 * t : 8 * t + FIELDS, :] = ghosts[t]
            message[where[e], 8 * t + FIELDS : 8 * t + 8, :] = packed[2 * t : 2 * t + 2, :]


def near_part(plan, field, diag, own, slot, table, image, seen, push, left, hot):
    rows = plan.near_tiles
    tiles = [field[:, s * LANES : (s + 1) * LANES] for s in range(plan.grain_tiles)]
    for side, index in enumerate((own, slot)):
        for t in range(rows):
            at = (side * rows + t) * 8
            seen[at : at + 8, :] = lane_gather(tiles, spread(index, t))
    first = [row_of(seen, c, 8, rows) for c in range(FIELDS)]
    second = [row_of(seen, rows * 8 + c, 8, rows) for c in range(FIELDS)]
    consts = [table[k, 0:rows, :] for k in range(9)]
    force, lever, moment = response(first, second, consts)
    for c in range(3):
        push[pl.ds(c, rows, stride=8), :] = force[c]
        push[pl.ds(3 + c, rows, stride=8), :] = consts[3] * lever[c] + moment[c]
        push[pl.ds(rows * 8 + c, rows, stride=8), :] = -force[c]
        push[pl.ds(rows * 8 + 3 + c, rows, stride=8), :] = consts[4] * lever[c] - moment[c]
    zero = jnp.zeros((2 * rows, LANES), jnp.float32)
    for c in range(FIELDS, 8):
        push[pl.ds(c, 2 * rows, stride=8), :] = zero
    parts = plan.grains // plan.rim
    grain = lax.broadcasted_iota(jnp.int32, (plan.rim, LANES), 0)
    for side, index in enumerate((own, slot)):
        for t in range(rows):
            at = side * rows + t
            value = push[at * 8 : at * 8 + 8, :]
            part = lax.div(spread(index, t), plan.rim)
            lanes = slice(at * LANES, (at + 1) * LANES)
            lows = []
            for q in range(parts):
                pair, low = three_parts(jnp.where(part == q, value, 0.0))
                left[q * 16 : q * 16 + 16, lanes] = pair
                lows.append(low)
            for q in range(0, parts, 2):
                left[parts * 16 + q * 8 : parts * 16 + q * 8 + 16, lanes] = jnp.concatenate(
                    lows[q : q + 2], axis=0
                )
            low = jnp.bitwise_and(index[t : t + 1, :], plan.rim - 1)
            hot[:, lanes] = jnp.where(grain == low, 1.0, 0.0).astype(jnp.bfloat16)
    total = lax.dot_general(
        left[...], hot[...], (((1,), (1,)), ((), ())), preferred_element_type=jnp.float32
    )
    for q in range(parts):
        lanes = slice(q * plan.rim, (q + 1) * plan.rim)
        at = parts * 16 + q * 8
        force = total[at : at + 8, :] + total[q * 16 + 8 : q * 16 + 16, :]
        force = force + total[q * 16 : q * 16 + 8, :]
        image[:, lanes] = diag[:, lanes] * field[:, lanes] - force


def near_first(
    plan, stiff_h, own_h, slot_h, kind_h, normal_h, radii_h, rhs_h, diag_h,
    image, table, field, diag, own, slot, stiff, kind, radii, rhs, ground, seen, push, left, hot, sems,
):
    rows = plan.near_tiles
    copies = fetch(
        [
            (stiff_h, stiff),
            (own_h, own),
            (slot_h, slot),
            (kind_h, kind),
            (radii_h.at[0, 0, 0], radii),
            (rhs_h, rhs),
            (diag_h, ground),
        ]
        + [(normal_h.at[pl.ds(c * plan.tiles, plan.tiles), :], table.at[c]) for c in range(3)],
        sems,
    )
    for copy in copies:
        copy.wait()
    for source, target in ((rhs, field), (ground, diag)):
        target[FIELDS:, :] = jnp.zeros((8 - FIELDS, plan.grains), jnp.float32)
        for t in range(plan.grain_tiles):
            target[0:FIELDS, t * LANES : (t + 1) * LANES] = row_of(
                source, t, plan.grain_tiles, FIELDS
            )
    for t in range(rows):
        lanes = slice(t * LANES, (t + 1) * LANES)
        for c in range(2):
            table[3 + c, t : t + 1, :] = radii[c : c + 1, lanes]
    lane = lax.broadcasted_iota(jnp.int32, (rows, LANES), 1)
    line = lax.broadcasted_iota(jnp.int32, (rows, LANES), 0)
    valid = line * LANES + lane < plan.near
    for k, value in enumerate(coefficients(stiff, kind[0:rows, :], plan.types, valid)):
        table[5 + k, 0:rows, :] = value
    near_part(plan, field, diag, own, slot, table, image, seen, push, left, hot)


def far_forces(plan, local, there, table, hot, push, left):
    rows = plan.far
    first = [row_of(local, c, 8, rows) for c in range(FIELDS)]
    second = [row_of(there, c, 8, rows) for c in range(FIELDS)]
    consts = [table[k, 0:rows, :] for k in range(9)]
    force, lever, moment = response(first, second, consts)
    for c in range(3):
        push[pl.ds(c, rows, stride=8), :] = force[c]
        push[pl.ds(3 + c, rows, stride=8), :] = consts[3] * lever[c] + moment[c]
    zero = jnp.zeros((rows, LANES), jnp.float32)
    for c in range(FIELDS, 8):
        push[pl.ds(c, rows, stride=8), :] = zero
    for e in range(rows):
        lanes = slice(e * LANES, (e + 1) * LANES)
        pair, low = three_parts(push[e * 8 : e * 8 + 8, :])
        left[0:16, lanes] = pair
        left[16:32, lanes] = jnp.concatenate([low, jnp.zeros_like(low)], axis=0)
    total = jnp.dot(left[...], hot[...], preferred_element_type=jnp.float32)
    return total[0:8, :] + (total[8:16, :] + total[16:24, :])


def send_rim(plan, field, index, sums, message, local):
    row = lax.broadcasted_iota(jnp.int32, (8, LANES), 0)
    base = jnp.where(row == FIELDS, sums[0], jnp.where(row == FIELDS + 1, sums[1], 0.0))
    message[...] = jnp.broadcast_to(base[None], message.shape)
    tiles = [field[:, t * LANES : (t + 1) * LANES] for t in range(plan.rim_tiles)]
    where = plan.neighbours()
    for e in range(plan.far):
        tile = lane_gather(tiles, spread(index, e))
        local[e * 8 : e * 8 + 8, :] = tile
        message[where[e], :, :] = jnp.where(row < FIELDS, pltpu.roll(tile, plan.half, 1), base)


def partial_sum(left, right):
    product = left * right
    total = product[:, 0:LANES]
    for t in range(1, product.shape[1] // LANES):
        total = total + product[:, t * LANES : (t + 1) * LANES]
    return jnp.sum(total, axis=0, keepdims=True)


def full_sum(received, row):
    return jnp.sum(jnp.sum(received[:, row, :], axis=0, keepdims=True), axis=1, keepdims=True)


def far_first(
    plan, stiff, received, mine, field, image,
    w, message, table, index, hot, local, merged, there, push, left,
):
    lane8 = lax.broadcasted_iota(jnp.int32, (8, LANES), 1)
    where = plan.neighbours()
    rows = plan.far
    for e in range(rows):
        own = pltpu.roll(mine[e * 8 : e * 8 + 8, :], plan.half, 1)
        packed = jnp.concatenate(
            [
                received[where[e], 8 * t + FIELDS : 8 * t + 8, :]
                for t in range(plan.rim_tiles)
            ],
            axis=0,
        )
        chunk = jnp.concatenate([packed, pltpu.roll(packed, plan.half, 1)], axis=0)
        merged[e * 8 : e * 8 + 8, :] = jnp.where(lane8 < plan.half, chunk, own)
    mirror = lax.broadcasted_iota(jnp.int32, (rows, LANES), 1) < plan.half
    row = [row_of(merged, r, 8, rows) for r in range(8)]
    for c in range(3):
        table[c, 0:rows, :] = jnp.where(mirror, -row[3 + c], row[3 + c])
    table[3, 0:rows, :] = jnp.where(mirror, row[7], row[6])
    table[4, 0:rows, :] = jnp.where(mirror, row[6], row[7])
    for k, value in enumerate(coefficients(stiff, row[2], plan.types)):
        table[5 + k, 0:rows, :] = value
    here = jnp.where(mirror, row[1], row[0])
    away = jnp.where(mirror, row[0], row[1]).astype(jnp.int32)
    index[0:rows, :] = here.astype(jnp.int32)
    make = one_hot(here, plan.rim)
    tiles = [field[:, t * LANES : (t + 1) * LANES] for t in range(plan.rim_tiles)]
    for e in range(rows):
        hot[e * LANES : (e + 1) * LANES, :] = make(e)
        local[e * 8 : e * 8 + 8, :] = lane_gather(tiles, spread(index, e))
        ghosts = [received[where[e], 8 * t : 8 * t + 8, :] for t in range(plan.rim_tiles)]
        there[e * 8 : e * 8 + 8, :] = lane_gather(
            ghosts, jnp.broadcast_to(away[e : e + 1, :], (8, LANES))
        )
    force = far_forces(plan, local, there, table, hot, push, left)
    w[...] = image[...]
    w[:, 0 : plan.rim] = image[:, 0 : plan.rim] - force
    r = field[...]
    sums = (partial_sum(r, r), partial_sum(w[...], r))
    send_rim(plan, w, index, sums, message, local)


def far_step(plan, number, *refs):
    refs = list(refs)

    def take(count):
        return [refs.pop(0) for _ in range(count)]

    received, image, table, index, hot, local, r, w = take(8)
    if number:
        p, s, z, x, past = take(5)
    last = number == ITERS - 2
    r_new, p_new, s_new, x_new, w_new, past_new = take(6)
    if not last:
        z_new, message, local_new = take(3)
    else:
        (message,) = take(1)
    there, push, left = take(3)

    where = plan.neighbours()
    for e in range(plan.far):
        there[e * 8 : e * 8 + 8, :] = received[where[e], :, :]
    gamma = full_sum(received, FIELDS)
    delta = full_sum(received, FIELDS + 1)
    force = far_forces(plan, local, there, table, hot, push, left)
    q = jnp.concatenate(
        [image[:, 0 : plan.rim] - force, image[:, plan.rim :]], axis=1
    )
    if number:
        beta = gamma / past[0:1, 0:1]
        alpha = gamma / (delta - beta * gamma / past[1:2, 0:1])
        z_now = q + beta * z[...]
        s_now = w[...] + beta * s[...]
        p_now = r[...] + beta * p[...]
        x_new[...] = x[...] + alpha * p_now
    else:
        alpha = gamma / delta
        z_now = q
        s_now = w[...]
        p_now = r[...]
        x_new[...] = alpha * p_now
    r_now = r[...] - alpha * s_now
    w_now = w[...] - alpha * z_now
    r_new[...] = r_now
    w_new[...] = w_now
    p_new[...] = p_now
    s_new[...] = s_now
    past_new[0:1, :] = jnp.broadcast_to(gamma, (1, LANES))
    past_new[1:2, :] = jnp.broadcast_to(alpha, (1, LANES))
    sums = (partial_sum(r_now, r_now), partial_sum(w_now, r_now))
    if not last:
        z_new[...] = z_now
        send_rim(plan, w_new, index, sums, message, local_new)
    else:
        base = jnp.concatenate(sums, axis=0)
        message[...] = jnp.broadcast_to(base[None], message.shape)


def finish(plan, received, r, w, p, s, x, past, x_out, r_out, x_last, r_last, sems):
    gamma = full_sum(received, 0)
    delta = full_sum(received, 1)
    beta = gamma / past[0:1, 0:1]
    alpha = gamma / (delta - beta * gamma / past[1:2, 0:1])
    for t in range(plan.grain_tiles):
        here = slice(0, FIELDS), slice(t * LANES, (t + 1) * LANES)
        there = pl.ds(t, FIELDS, stride=plan.grain_tiles), slice(None)
        x_last[there] = x[here] + alpha * (r[here] + beta * p[here])
        r_last[there] = r[here] - alpha * (w[here] + beta * s[here])
    for copy in fetch([(x_last, x_out), (r_last, r_out)], sems):
        copy.wait()


def shards(
    mesh,
    right_side,
    grain_diag,
    stiffness,
    contact_own,
    contact_slot,
    contact_type,
    contact_normal,
    contact_radii,
):
    plan = Plan(mesh, right_side.shape[-1], contact_own.shape[-1], stiffness.shape[1])
    own = contact_own.reshape(plan.tiles, LANES)
    slot = contact_slot.reshape(plan.tiles, LANES)
    kind = contact_type.reshape(plan.tiles, LANES)
    normal = contact_normal.reshape(3 * plan.tiles, LANES)
    lines = (FIELDS * plan.grain_tiles, LANES)
    rhs = right_side.reshape(lines)
    ground = grain_diag.reshape(lines)
    f32, bf16, i32 = jnp.float32, jnp.bfloat16, jnp.int32
    vmem, hbm, dma = pltpu.MemorySpace.VMEM, pltpu.MemorySpace.HBM, pltpu.SemaphoreType.DMA
    wide = (8, plan.grains)
    far = (plan.far * 8, LANES)
    far_table = (9, -(-plan.far // 8) * 8, LANES)
    near_table = (9, plan.tiles, LANES)
    table = (plan.tiles, LANES)
    near_rows = 2 * plan.near_tiles
    parts = plan.grains // plan.rim
    rest = plan.contacts - plan.near // LANES * LANES

    def call(body, outs, scratch, *args, raw=False, end=False):
        space = hbm if raw else vmem
        args = [pltpu.with_memory_space_constraint(x, space) for x in args]
        return pl.pallas_call(
            functools.partial(body, plan),
            out_shape=[(hbm if end else vmem)(dims, dtype) for dims, dtype in outs],
            in_specs=[pl.BlockSpec(memory_space=space)] * len(args),
            out_specs=[pl.BlockSpec(memory_space=hbm if end else vmem)] * len(outs),
            scratch_shapes=scratch,
            compiler_params=pltpu.CompilerParams(vmem_limit_bytes=16 * 2**20),
        )(*args)

    def exchange(message):
        return lax.all_to_all(message, AXES, 0, 0)

    tile = (plan.devices, 8, LANES)
    near_scratch = [
        vmem((near_rows * 8, LANES), f32),
        vmem((near_rows * 8, LANES), f32),
        vmem((parts * 24, near_rows * LANES), bf16),
        vmem((plan.rim, near_rows * LANES), bf16),
    ]
    far_scratch = [vmem(far, f32), vmem(far, f32), vmem((32, plan.far * LANES), bf16)]

    message, mine = call(
        send_setup,
        [((plan.devices, 8 * plan.rim_tiles, LANES), f32), (far, f32)],
        [
            vmem(table, i32),
            vmem(table, i32),
            vmem(table, i32),
            vmem(normal.shape, f32),
            vmem((2, rest), f32),
            vmem(lines, f32),
            vmem((rest // LANES * 8, LANES), f32),
            dma((6,)),
        ],
        own, slot, kind, normal, contact_radii, rhs,
        raw=True,
    )
    received = exchange(message)
    image, near_const, field, diag, own, slot, stiff = call(
        near_first,
        [
            (wide, f32),
            (near_table, f32),
            (wide, f32),
            (wide, f32),
            (table, i32),
            (table, i32),
            (stiffness.shape, f32),
        ],
        [vmem(table, i32), vmem((2, plan.contacts), f32), vmem(lines, f32), vmem(lines, f32)]
        + near_scratch
        + [dma((10,))],
        stiffness, own, slot, kind, normal, contact_radii, rhs, ground,
        raw=True,
    )
    w, message, far_const, index, far_hot, local = call(
        far_first,
        [
            (wide, f32),
            (tile, f32),
            (far_table, f32),
            (far_table[1:], i32),
            ((plan.far * LANES, plan.rim), bf16),
            (far, f32),
        ],
        [vmem(far, f32)] + far_scratch,
        stiff, received, mine, field, image,
    )
    r = field
    state = ()
    for number in range(ITERS - 1):
        received = exchange(message)
        (image,) = call(
            near_part,
            [(wide, f32)],
            near_scratch,
            w, diag, own, slot, near_const,
        )
        last = number == ITERS - 2
        outs = [(wide, f32)] * 5 + [((8, LANES), f32)]
        if last:
            outs = outs + [((plan.devices, 2, LANES), f32)]
        else:
            outs = outs + [(wide, f32), (tile, f32), (far, f32)]
        made = call(
            lambda plan, *refs, number=number: far_step(plan, number, *refs),
            outs,
            far_scratch,
            received, image, far_const, index, far_hot, local, r, w, *state,
        )
        r, p, s, x, w, past = made[:6]
        if last:
            message = made[6]
        else:
            z, message, local = made[6:]
            state = (p, s, z, x, past)
    received = exchange(message)
    solution_field, residual = call(
        finish,
        [(lines, f32)] * 2,
        [vmem(lines, f32), vmem(lines, f32), dma((2,))],
        received, r, w, p, s, x, past,
        end=True,
    )
    return (solution_field.reshape(right_side.shape), residual.reshape(right_side.shape))


def solution(mesh):
    vector = P("gx", "gy", "gz", None)
    matrix = P("gx", "gy", "gz", None, None)
    return jax.shard_map(
        functools.partial(shards, mesh),
        mesh=mesh,
        in_specs=(matrix, matrix, P(), vector, vector, vector, matrix, matrix),
        out_specs=(matrix, matrix),
        check_vma=False,
    )
```

```python
import functools

import jax
import jax.numpy as jnp
from jax import lax
from jax.experimental import pallas as pl
from jax.experimental.pallas import tpu as pltpu
from jax.sharding import PartitionSpec as P

ITERS = 4
AXES = ("gx", "gy", "gz")
LANES = 128
FIELDS = 6


class Plan:
    def __init__(self, mesh, grains, contacts, types):
        self.counts = tuple(mesh.shape[axis] for axis in AXES)
        self.devices = self.counts[0] * self.counts[1] * self.counts[2]
        self.grains = grains
        self.rim = grains // 4
        self.rim_bits = self.rim.bit_length() - 1
        self.group = grains // 32
        self.contacts = contacts
        self.types = types
        self.near = contacts - 26 * self.group
        self.near_tiles = -(-self.near // LANES)
        middle = self.near_tiles // 16 * 8
        self.near_groups = [(0, middle), (middle, self.near_tiles)] if middle else [(0, self.near_tiles)]
        self.tiles = contacts // LANES
        self.grain_tiles = grains // LANES
        self.rim_tiles = self.rim // LANES
        sides = {}
        for k in range(26):
            whole = k + (1 if k >= 13 else 0)
            offset = (whole // 9 - 1, whole // 3 % 3 - 1, whole % 3 - 1)
            delta = tuple(o % c for o, c in zip(offset, self.counts))
            sides.setdefault(delta, []).append(k)
        self.sides = sorted(sides.items())
        self.far = len(self.sides)
        most = max(len(groups) for groups in sides.values())
        self.half = -(-most * self.group // (LANES // 2)) * (LANES // 2)
        assert self.half * 2 == LANES

    def neighbours(self):
        place = [lax.axis_index(axis) for axis in AXES]
        found = []
        for delta, _ in self.sides:
            x, y, z = (lax.rem(p + d, c) for p, d, c in zip(place, delta, self.counts))
            found.append((x * self.counts[1] + y) * self.counts[2] + z)
        return found


def row_of(ref, row, stride, count):
    return ref[pl.ds(row, count, stride=stride), :]


def lane_gather(tiles, index):
    low = jnp.bitwise_and(index, LANES - 1)
    high = lax.shift_right_logical(index, 7)
    total = jnp.zeros(tiles[0].shape, tiles[0].dtype)
    for which, tile in enumerate(tiles):
        found = jnp.take_along_axis(tile, low, axis=1, mode="promise_in_bounds")
        total = jnp.where(high == which, found, total)
    return total


def spread(ref, row):
    return jnp.broadcast_to(ref[row : row + 1, :], (8, LANES))


def coefficients(stiff_ref, kind, types, valid=None):
    found = []
    for which in range(4):
        total = jnp.zeros(kind.shape, jnp.float32)
        for t in range(types):
            total = jnp.where(kind == t, stiff_ref[which : which + 1, t : t + 1], total)
        if valid is not None:
            total = jnp.where(valid, total, 0.0)
        found.append(total)
    normal_k, shear_k, roll_k, twist_k = found
    return shear_k, normal_k - shear_k, roll_k, twist_k - roll_k


def response(first, second, table):
    n = table[0:3]
    first_r, second_r, shear_k, normal_d, roll_k, twist_d = table[3:]
    p = [second_r * second[3 + c] + first_r * first[3 + c] for c in range(3)]
    delta = []
    for c in range(3):
        a, b = (c + 1) % 3, (c + 2) % 3
        delta.append(second[c] - first[c] - (p[a] * n[b] - p[b] * n[a]))
    theta = [second[3 + c] - first[3 + c] for c in range(3)]
    along = normal_d * (n[0] * delta[0] + n[1] * delta[1] + n[2] * delta[2])
    twist = twist_d * (n[0] * theta[0] + n[1] * theta[1] + n[2] * theta[2])
    force = [shear_k * delta[c] + along * n[c] for c in range(3)]
    moment = [roll_k * theta[c] + twist * n[c] for c in range(3)]
    lever = []
    for c in range(3):
        a, b = (c + 1) % 3, (c + 2) % 3
        lever.append(n[a] * force[b] - n[b] * force[a])
    return force, lever, moment


def three_parts(value):
    high = value.astype(jnp.bfloat16).astype(jnp.float32)
    rest = value - high
    middle = rest.astype(jnp.bfloat16).astype(jnp.float32)
    return high, middle, rest - middle


def stacked(upper, lower):
    return jnp.concatenate([upper, lower], axis=0).astype(jnp.bfloat16)


def fetch(copies, sems):
    started = [
        pltpu.make_async_copy(source, target, sems.at[i])
        for i, (source, target) in enumerate(copies)
    ]
    for copy in started:
        copy.start()
    return started


def one_hot(index_tile, width):
    rows = index_tile.shape[0]
    padded = index_tile
    if rows < LANES:
        padded = jnp.concatenate(
            [index_tile, jnp.zeros((LANES - rows, LANES), index_tile.dtype)], axis=0
        )
    turned = jnp.transpose(padded)
    lane = lax.broadcasted_iota(jnp.int32, (LANES, width), 1).astype(jnp.float32)

    def make(row):
        return jnp.where(turned[:, row : row + 1] == lane, 1.0, 0.0).astype(jnp.bfloat16)

    return make


def send_setup(
    plan, own_h, slot_h, kind_h, normal_h, radii_h, rhs_h,
    message, mine, own, slot, kind, normal, radii, rhs, stack, sems,
):
    first = plan.near // LANES
    lanes = pl.ds(first * LANES, plan.contacts - first * LANES)
    for copy in fetch(
        [
            (own_h, own),
            (slot_h, slot),
            (kind_h, kind),
            (normal_h, normal),
            (radii_h.at[0, 0, 0, :, lanes], radii),
            (rhs_h, rhs),
        ],
        sems,
    ):
        copy.wait()
    for t in range(first, plan.tiles):
        at = (t - first) * 8
        lanes = slice(at * 16, at * 16 + LANES)
        stack[at : at + 1, :] = own[t : t + 1, :].astype(jnp.float32)
        stack[at + 1 : at + 2, :] = jnp.bitwise_and(slot[t : t + 1, :], plan.rim - 1).astype(
            jnp.float32
        )
        stack[at + 2 : at + 3, :] = kind[t : t + 1, :].astype(jnp.float32)
        stack[at + 3 : at + 6, :] = row_of(normal, t, plan.tiles, 3)
        stack[at + 6 : at + 8, :] = radii[:, lanes]
    lane = lax.broadcasted_iota(jnp.int32, (8, LANES), 1)
    row = lax.broadcasted_iota(jnp.int32, (8, LANES), 0)
    where = plan.neighbours()
    ghosts = [row_of(rhs, t, plan.grain_tiles, FIELDS) for t in range(plan.rim_tiles)]
    for e, (_, groups) in enumerate(plan.sides):
        chunk = jnp.where(row == 2, float(plan.types), 0.0)
        for j, k in enumerate(groups):
            place = plan.near + k * plan.group
            t, inside = place // LANES, place % LANES
            tile = stack[(t - first) * 8 : (t - first) * 8 + 8, :]
            turn = (j * plan.group - inside) % LANES
            if turn:
                tile = pltpu.roll(tile, turn, 1)
            here = (lane >= j * plan.group) & (lane < (j + 1) * plan.group)
            chunk = jnp.where(here, tile, chunk)
        mine[e * 8 : e * 8 + 8, :] = chunk
        packed = jnp.where(lane < plan.half, chunk, pltpu.roll(pltpu.roll(chunk, 4, 0), plan.half, 1))
        for t in range(plan.rim_tiles):
            message[where[e], 8 * t : 8 * t + FIELDS, :] = ghosts[t]
            message[where[e], 8 * t + FIELDS : 8 * t + 8, :] = packed[2 * t : 2 * t + 2, :]


def near_part(plan, field, diag, own, slot, table, hot, image, seen, push, left):
    tiles = [field[:, s * LANES : (s + 1) * LANES] for s in range(plan.grain_tiles)]
    parts = plan.grains // plan.rim
    total = None
    for start, stop in plan.near_groups:
        rows = stop - start
        base = 2 * start
        for side, index in enumerate((own, slot)):
            for t in range(rows):
                at = (base + side * rows + t) * 8
                seen[at : at + 8, :] = lane_gather(tiles, spread(index, start + t))
        one, two = base * 8, (base + rows) * 8
        first = [row_of(seen, one + c, 8, rows) for c in range(FIELDS)]
        second = [row_of(seen, two + c, 8, rows) for c in range(FIELDS)]
        consts = [table[k, start:stop, :] for k in range(9)]
        force, lever, moment = response(first, second, consts)
        zero = jnp.zeros((rows, LANES), jnp.float32)
        for c in range(3):
            push[pl.ds(one + c, rows, stride=8), :] = force[c]
            push[pl.ds(one + 3 + c, rows, stride=8), :] = consts[3] * lever[c] + moment[c]
            push[pl.ds(two + c, rows, stride=8), :] = -force[c]
            push[pl.ds(two + 3 + c, rows, stride=8), :] = consts[4] * lever[c] - moment[c]
        for c in range(FIELDS, 8):
            push[pl.ds(one + c, rows, stride=8), :] = zero
            push[pl.ds(two + c, rows, stride=8), :] = zero
        for side, index in enumerate((own, slot)):
            for t in range(rows):
                at = base + side * rows + t
                lanes = slice(at * LANES, (at + 1) * LANES)
                split = three_parts(push[at * 8 : at * 8 + 8, :])
                part = lax.shift_right_logical(spread(index, start + t), plan.rim_bits)
                lows = []
                for q in range(parts):
                    here = part == q
                    high, middle, low = [jnp.where(here, x, 0.0) for x in split]
                    left[q * 16 : q * 16 + 16, lanes] = stacked(high, middle)
                    lows.append(low)
                for q in range(0, parts, 2):
                    left[parts * 16 + q * 8 : parts * 16 + q * 8 + 16, lanes] = stacked(
                        lows[q], lows[q + 1]
                    )
        lanes = slice(base * LANES, (base + 2 * rows) * LANES)
        sums = jnp.dot(left[:, lanes], hot[lanes, :], preferred_element_type=jnp.float32)
        total = sums if total is None else total + sums
    for q in range(parts):
        lanes = slice(q * plan.rim, (q + 1) * plan.rim)
        at = parts * 16 + q * 8
        force = total[at : at + 8, :] + total[q * 16 + 8 : q * 16 + 16, :]
        force = force + total[q * 16 : q * 16 + 8, :]
        image[:, lanes] = diag[:, lanes] * field[:, lanes] - force


def near_first(
    plan, stiff_h, own_h, slot_h, kind_h, normal_h, radii_h, rhs_h, diag_h,
    image, table, field, diag, own, slot, stiff, hot, kind, radii, rhs, ground, seen, push, left, sems,
):
    rows = plan.near_tiles
    copies = fetch(
        [
            (stiff_h, stiff),
            (own_h, own),
            (slot_h, slot),
            (kind_h, kind),
            (radii_h.at[0, 0, 0], radii),
            (rhs_h, rhs),
            (diag_h, ground),
        ]
        + [(normal_h.at[pl.ds(c * plan.tiles, plan.tiles), :], table.at[c]) for c in range(3)],
        sems,
    )
    for copy in copies:
        copy.wait()
    for source, target in ((rhs, field), (ground, diag)):
        target[FIELDS:, :] = jnp.zeros((8 - FIELDS, plan.grains), jnp.float32)
        for t in range(plan.grain_tiles):
            target[0:FIELDS, t * LANES : (t + 1) * LANES] = row_of(
                source, t, plan.grain_tiles, FIELDS
            )
    for t in range(rows):
        lanes = slice(t * LANES, (t + 1) * LANES)
        for c in range(2):
            table[3 + c, t : t + 1, :] = radii[c : c + 1, lanes]
    lane = lax.broadcasted_iota(jnp.int32, (rows, LANES), 1)
    line = lax.broadcasted_iota(jnp.int32, (rows, LANES), 0)
    valid = line * LANES + lane < plan.near
    for k, value in enumerate(coefficients(stiff, kind[0:rows, :], plan.types, valid)):
        table[5 + k, 0:rows, :] = value
    for side, index in enumerate((own, slot)):
        low = jnp.bitwise_and(index[...], plan.rim - 1).astype(jnp.float32)
        make = one_hot(low, plan.rim)
        for start, stop in plan.near_groups:
            for t in range(start, stop):
                at = (2 * start + side * (stop - start) + t - start) * LANES
                hot[at : at + LANES, :] = make(t)
    near_part(plan, field, diag, own, slot, table, hot, image, seen, push, left)


def far_forces(plan, local, there, table, hot, push, left):
    rows = plan.far
    first = [row_of(local, c, 8, rows) for c in range(FIELDS)]
    second = [row_of(there, c, 8, rows) for c in range(FIELDS)]
    consts = [table[k, 0:rows, :] for k in range(9)]
    force, lever, moment = response(first, second, consts)
    for c in range(3):
        push[pl.ds(c, rows, stride=8), :] = force[c]
        push[pl.ds(3 + c, rows, stride=8), :] = consts[3] * lever[c] + moment[c]
    zero = jnp.zeros((rows, LANES), jnp.float32)
    for c in range(FIELDS, 8):
        push[pl.ds(c, rows, stride=8), :] = zero
    for e in range(rows):
        lanes = slice(e * LANES, (e + 1) * LANES)
        high, middle, low = three_parts(push[e * 8 : e * 8 + 8, :])
        left[0:16, lanes] = stacked(high, middle)
        left[16:32, lanes] = stacked(low, jnp.zeros_like(low))
    total = jnp.dot(left[...], hot[...], preferred_element_type=jnp.float32)
    return total[0:8, :] + (total[8:16, :] + total[16:24, :])


def send_rim(plan, field, index, sums, message, local):
    row = lax.broadcasted_iota(jnp.int32, (8, LANES), 0)
    base = jnp.where(row == FIELDS, sums[0], jnp.where(row == FIELDS + 1, sums[1], 0.0))
    message[...] = jnp.broadcast_to(base[None], message.shape)
    tiles = [field[:, t * LANES : (t + 1) * LANES] for t in range(plan.rim_tiles)]
    where = plan.neighbours()
    for e in range(plan.far):
        tile = lane_gather(tiles, spread(index, e))
        local[e * 8 : e * 8 + 8, :] = tile
        message[where[e], :, :] = jnp.where(row < FIELDS, pltpu.roll(tile, plan.half, 1), base)


def partial_sums(r, w, s=None, p=None):
    def fold(product):
        total = product[:, 0:LANES]
        for t in range(1, product.shape[1] // LANES):
            total = total + product[:, t * LANES : (t + 1) * LANES]
        return total

    def join(left, right):
        low = lax.broadcasted_iota(jnp.int32, (8, LANES), 1) < LANES // 2
        halves = [x + pltpu.roll(x, LANES // 2, 1) for x in (left, right)]
        return jnp.sum(jnp.where(low, *halves), axis=0, keepdims=True)

    if s is None:
        zero = jnp.zeros((8, LANES), jnp.float32)
        return join(fold(r * r), zero), join(fold(w * r), zero)
    return join(fold(r * r), fold(r * s + p * w)), join(fold(w * r), fold(p * s))


def full_sums(received, first):
    low = lax.broadcasted_iota(jnp.int32, (1, LANES), 1) < LANES // 2
    found = []
    for row in (first, first + 1):
        total = jnp.sum(received[:, row, :], axis=0, keepdims=True)
        for half in (jnp.where(low, total, 0.0), jnp.where(low, 0.0, total)):
            found.append(jnp.sum(half, axis=1, keepdims=True))
    return found[0], found[2], found[1], found[3]


def step_sizes(sums, past):
    gamma, delta, mixed, energy = sums
    beta = gamma / past[0:1, 0:1]
    return gamma / (delta + beta * (mixed + beta * energy)), beta


def far_first(
    plan, stiff, received, mine, field, image,
    w, message, table, index, hot, local, merged, there, push, left,
):
    lane8 = lax.broadcasted_iota(jnp.int32, (8, LANES), 1)
    where = plan.neighbours()
    rows = plan.far
    for e in range(rows):
        own = pltpu.roll(mine[e * 8 : e * 8 + 8, :], plan.half, 1)
        packed = jnp.concatenate(
            [
                received[where[e], 8 * t + FIELDS : 8 * t + 8, :]
                for t in range(plan.rim_tiles)
            ],
            axis=0,
        )
        chunk = jnp.concatenate([packed, pltpu.roll(packed, plan.half, 1)], axis=0)
        merged[e * 8 : e * 8 + 8, :] = jnp.where(lane8 < plan.half, chunk, own)
    mirror = lax.broadcasted_iota(jnp.int32, (rows, LANES), 1) < plan.half
    row = [row_of(merged, r, 8, rows) for r in range(8)]
    for c in range(3):
        table[c, 0:rows, :] = jnp.where(mirror, -row[3 + c], row[3 + c])
    table[3, 0:rows, :] = jnp.where(mirror, row[7], row[6])
    table[4, 0:rows, :] = jnp.where(mirror, row[6], row[7])
    for k, value in enumerate(coefficients(stiff, row[2], plan.types)):
        table[5 + k, 0:rows, :] = value
    here = jnp.where(mirror, row[1], row[0])
    away = jnp.where(mirror, row[0], row[1]).astype(jnp.int32)
    index[0:rows, :] = here.astype(jnp.int32)
    make = one_hot(here, plan.rim)
    tiles = [field[:, t * LANES : (t + 1) * LANES] for t in range(plan.rim_tiles)]
    for e in range(rows):
        hot[e * LANES : (e + 1) * LANES, :] = make(e)
        local[e * 8 : e * 8 + 8, :] = lane_gather(tiles, spread(index, e))
        ghosts = [received[where[e], 8 * t : 8 * t + 8, :] for t in range(plan.rim_tiles)]
        there[e * 8 : e * 8 + 8, :] = lane_gather(
            ghosts, jnp.broadcast_to(away[e : e + 1, :], (8, LANES))
        )
    force = far_forces(plan, local, there, table, hot, push, left)
    w[...] = image[...]
    w[:, 0 : plan.rim] = image[:, 0 : plan.rim] - force
    sums = partial_sums(field[...], w[...])
    send_rim(plan, w, index, sums, message, local)


def far_step(plan, number, *refs):
    refs = list(refs)

    def take(count):
        return [refs.pop(0) for _ in range(count)]

    received, diag, own, slot, near_const, near_hot, table, index, hot, local, r, w = take(12)
    if number:
        p, s, z, x, past = take(5)
    last = number == ITERS - 2
    r_new, p_new, s_new, x_new, w_new, past_new = take(6)
    if not last:
        z_new, message, local_new = take(3)
    else:
        (message,) = take(1)
    image, near_seen, near_push, near_left, there, push, left = take(7)
    near_part(plan, w, diag, own, slot, near_const, near_hot, image, near_seen, near_push, near_left)

    where = plan.neighbours()
    for e in range(plan.far):
        there[e * 8 : e * 8 + 8, :] = received[where[e], :, :]
    sums = full_sums(received, FIELDS)
    force = far_forces(plan, local, there, table, hot, push, left)
    q = jnp.concatenate(
        [image[:, 0 : plan.rim] - force, image[:, plan.rim :]], axis=1
    )
    if number:
        alpha, beta = step_sizes(sums, past)
        z_now = q + beta * z[...]
        s_now = w[...] + beta * s[...]
        p_now = r[...] + beta * p[...]
        x_new[...] = x[...] + alpha * p_now
    else:
        alpha = sums[0] / sums[1]
        z_now = q
        s_now = w[...]
        p_now = r[...]
        x_new[...] = alpha * p_now
    r_now = r[...] - alpha * s_now
    w_now = w[...] - alpha * z_now
    r_new[...] = r_now
    w_new[...] = w_now
    p_new[...] = p_now
    s_new[...] = s_now
    past_new[...] = jnp.broadcast_to(sums[0], past_new.shape)
    sums = partial_sums(r_now, w_now, s_now, p_now)
    if not last:
        z_new[...] = z_now
        send_rim(plan, w_new, index, sums, message, local_new)
    else:
        base = jnp.concatenate(sums, axis=0)
        message[...] = jnp.broadcast_to(base[None], message.shape)


def finish(plan, received, r, w, p, s, x, past, x_out, r_out, x_last, r_last, sems):
    alpha, beta = step_sizes(full_sums(received, 0), past)
    for t in range(plan.grain_tiles):
        here = slice(0, FIELDS), slice(t * LANES, (t + 1) * LANES)
        there = pl.ds(t, FIELDS, stride=plan.grain_tiles), slice(None)
        x_last[there] = x[here] + alpha * (r[here] + beta * p[here])
        r_last[there] = r[here] - alpha * (w[here] + beta * s[here])
    for copy in fetch([(x_last, x_out), (r_last, r_out)], sems):
        copy.wait()


def shards(
    mesh,
    right_side,
    grain_diag,
    stiffness,
    contact_own,
    contact_slot,
    contact_type,
    contact_normal,
    contact_radii,
):
    plan = Plan(mesh, right_side.shape[-1], contact_own.shape[-1], stiffness.shape[1])
    own = contact_own.reshape(plan.tiles, LANES)
    slot = contact_slot.reshape(plan.tiles, LANES)
    kind = contact_type.reshape(plan.tiles, LANES)
    normal = contact_normal.reshape(3 * plan.tiles, LANES)
    lines = (FIELDS * plan.grain_tiles, LANES)
    rhs = right_side.reshape(lines)
    ground = grain_diag.reshape(lines)
    f32, bf16, i32 = jnp.float32, jnp.bfloat16, jnp.int32
    vmem, hbm, dma = pltpu.MemorySpace.VMEM, pltpu.MemorySpace.HBM, pltpu.SemaphoreType.DMA
    wide = (8, plan.grains)
    far = (plan.far * 8, LANES)
    far_table = (9, -(-plan.far // 8) * 8, LANES)
    near_table = (9, plan.tiles, LANES)
    table = (plan.tiles, LANES)
    near_rows = 2 * plan.near_tiles
    parts = plan.grains // plan.rim
    rest = plan.contacts - plan.near // LANES * LANES

    def call(body, outs, scratch, *args, raw=False, end=False):
        space = hbm if raw else vmem
        args = [pltpu.with_memory_space_constraint(x, space) for x in args]
        return pl.pallas_call(
            functools.partial(body, plan),
            out_shape=[(hbm if end else vmem)(dims, dtype) for dims, dtype in outs],
            in_specs=[pl.BlockSpec(memory_space=space)] * len(args),
            out_specs=[pl.BlockSpec(memory_space=hbm if end else vmem)] * len(outs),
            scratch_shapes=scratch,
            compiler_params=pltpu.CompilerParams(vmem_limit_bytes=16 * 2**20),
        )(*args)

    def exchange(message):
        return lax.all_to_all(message, AXES, 0, 0)

    tile = (plan.devices, 8, LANES)
    near_scratch = [
        vmem((near_rows * 8, LANES), f32),
        vmem((near_rows * 8, LANES), f32),
        vmem((parts * 24, near_rows * LANES), bf16),
    ]
    far_scratch = [vmem(far, f32), vmem(far, f32), vmem((32, plan.far * LANES), bf16)]

    message, mine = call(
        send_setup,
        [((plan.devices, 8 * plan.rim_tiles, LANES), f32), (far, f32)],
        [
            vmem(table, i32),
            vmem(table, i32),
            vmem(table, i32),
            vmem(normal.shape, f32),
            vmem((2, rest), f32),
            vmem(lines, f32),
            vmem((rest // LANES * 8, LANES), f32),
            dma((6,)),
        ],
        own, slot, kind, normal, contact_radii, rhs,
        raw=True,
    )
    received = exchange(message)
    image, near_const, field, diag, own, slot, stiff, near_hot = call(
        near_first,
        [
            (wide, f32),
            (near_table, f32),
            (wide, f32),
            (wide, f32),
            (table, i32),
            (table, i32),
            (stiffness.shape, f32),
            ((near_rows * LANES, plan.rim), bf16),
        ],
        [vmem(table, i32), vmem((2, plan.contacts), f32), vmem(lines, f32), vmem(lines, f32)]
        + near_scratch
        + [dma((10,))],
        stiffness, own, slot, kind, normal, contact_radii, rhs, ground,
        raw=True,
    )
    w, message, far_const, index, far_hot, local = call(
        far_first,
        [
            (wide, f32),
            (tile, f32),
            (far_table, f32),
            (far_table[1:], i32),
            ((plan.far * LANES, plan.rim), bf16),
            (far, f32),
        ],
        [vmem(far, f32)] + far_scratch,
        stiff, received, mine, field, image,
    )
    r = field
    state = ()
    for number in range(ITERS - 1):
        received = exchange(message)
        last = number == ITERS - 2
        outs = [(wide, f32)] * 5 + [((8, LANES), f32)]
        if last:
            outs = outs + [((plan.devices, 2, LANES), f32)]
        else:
            outs = outs + [(wide, f32), (tile, f32), (far, f32)]
        made = call(
            lambda plan, *refs, number=number: far_step(plan, number, *refs),
            outs,
            [vmem(wide, f32)] + near_scratch + far_scratch,
            received, diag, own, slot, near_const, near_hot, far_const, index, far_hot, local, r, w, *state,
        )
        r, p, s, x, w, past = made[:6]
        if last:
            message = made[6]
        else:
            z, message, local = made[6:]
            state = (p, s, z, x, past)
    received = exchange(message)
    solution_field, residual = call(
        finish,
        [(lines, f32)] * 2,
        [vmem(lines, f32), vmem(lines, f32), dma((2,))],
        received, r, w, p, s, x, past,
        end=True,
    )
    return (solution_field.reshape(right_side.shape), residual.reshape(right_side.shape))


def solution(mesh):
    vector = P("gx", "gy", "gz", None)
    matrix = P("gx", "gy", "gz", None, None)
    return jax.shard_map(
        functools.partial(shards, mesh),
        mesh=mesh,
        in_specs=(matrix, matrix, P(), vector, vector, vector, matrix, matrix),
        out_specs=(matrix, matrix),
        check_vma=False,
    )
```

```python
import functools

import jax
import jax.numpy as jnp
from jax import lax
from jax.experimental import pallas as pl
from jax.experimental.pallas import tpu as pltpu
from jax.sharding import PartitionSpec as P

ITERS = 4
AXES = ("gx", "gy", "gz")
LANES = 128
FIELDS = 6


class Plan:
    def __init__(self, mesh, grains, contacts, types):
        self.counts = tuple(mesh.shape[axis] for axis in AXES)
        self.devices = self.counts[0] * self.counts[1] * self.counts[2]
        self.grains = grains
        self.rim = grains // 4
        self.rim_bits = self.rim.bit_length() - 1
        self.group = grains // 32
        self.contacts = contacts
        self.types = types
        self.near = contacts - 26 * self.group
        self.near_tiles = -(-self.near // LANES)
        middle = self.near_tiles // 16 * 8
        self.near_groups = [(t, min(t + 8, self.near_tiles)) for t in range(0, self.near_tiles, 8)]
        self.tiles = contacts // LANES
        self.grain_tiles = grains // LANES
        self.rim_tiles = self.rim // LANES
        sides = {}
        for k in range(26):
            whole = k + (1 if k >= 13 else 0)
            offset = (whole // 9 - 1, whole // 3 % 3 - 1, whole % 3 - 1)
            delta = tuple(o % c for o, c in zip(offset, self.counts))
            sides.setdefault(delta, []).append(k)
        self.sides = sorted(sides.items())
        self.far = len(self.sides)
        most = max(len(groups) for groups in sides.values())
        self.half = -(-most * self.group // (LANES // 2)) * (LANES // 2)
        assert self.half * 2 == LANES

    def neighbours(self):
        place = [lax.axis_index(axis) for axis in AXES]
        found = []
        for delta, _ in self.sides:
            x, y, z = (lax.rem(p + d, c) for p, d, c in zip(place, delta, self.counts))
            found.append((x * self.counts[1] + y) * self.counts[2] + z)
        return found


def row_of(ref, row, stride, count):
    return ref[pl.ds(row, count, stride=stride), :]


def lane_gather(tiles, index):
    low = jnp.bitwise_and(index, LANES - 1)
    found = [jnp.take_along_axis(t, low, axis=1, mode="promise_in_bounds") for t in tiles]
    bit = LANES
    while len(found) > 1:
        odd = jnp.bitwise_and(index, bit) != 0
        found = [jnp.where(odd, b, a) for a, b in zip(found[0::2], found[1::2])]
        bit *= 2
    return found[0]


class Queue:
    def __init__(self):
        self.waiting = []

    def add(self, left, hot, sums, start, stop):
        step = 4 * LANES
        for at in range(start, stop, step):
            self.waiting.append((left, hot, sums, slice(at, min(at + step, stop))))

    def run(self, count=None):
        for _ in range(len(self.waiting) if count is None else min(count, len(self.waiting))):
            left, hot, sums, lanes = self.waiting.pop(0)
            sums.append(jnp.dot(left[:, lanes], hot[lanes, :], preferred_element_type=jnp.float32))
            if len(sums) == 2:
                sums[:] = [sums[0] + sums[1]]


def spread(ref, row):
    return jnp.broadcast_to(ref[row : row + 1, :], (8, LANES))


def coefficients(stiff_ref, kind, types, valid=None):
    found = []
    for which in range(4):
        total = jnp.zeros(kind.shape, jnp.float32)
        for t in range(types):
            total = jnp.where(kind == t, stiff_ref[which : which + 1, t : t + 1], total)
        if valid is not None:
            total = jnp.where(valid, total, 0.0)
        found.append(total)
    normal_k, shear_k, roll_k, twist_k = found
    return shear_k, normal_k - shear_k, roll_k, twist_k - roll_k


def response(first, second, table):
    n = table[0:3]
    first_r, second_r, shear_k, normal_d, roll_k, twist_d = table[3:]
    p = [second_r * second[3 + c] + first_r * first[3 + c] for c in range(3)]
    delta = []
    for c in range(3):
        a, b = (c + 1) % 3, (c + 2) % 3
        delta.append(second[c] - first[c] - (p[a] * n[b] - p[b] * n[a]))
    theta = [second[3 + c] - first[3 + c] for c in range(3)]
    along = normal_d * (n[0] * delta[0] + n[1] * delta[1] + n[2] * delta[2])
    twist = twist_d * (n[0] * theta[0] + n[1] * theta[1] + n[2] * theta[2])
    force = [shear_k * delta[c] + along * n[c] for c in range(3)]
    moment = [roll_k * theta[c] + twist * n[c] for c in range(3)]
    lever = []
    for c in range(3):
        a, b = (c + 1) % 3, (c + 2) % 3
        lever.append(n[a] * force[b] - n[b] * force[a])
    return force, lever, moment


def three_parts(value):
    high = value.astype(jnp.bfloat16).astype(jnp.float32)
    rest = value - high
    middle = rest.astype(jnp.bfloat16).astype(jnp.float32)
    return high, middle, rest - middle


def stacked(upper, lower):
    return jnp.concatenate([upper, lower], axis=0).astype(jnp.bfloat16)


def fetch(copies, sems):
    started = [
        pltpu.make_async_copy(source, target, sems.at[i])
        for i, (source, target) in enumerate(copies)
    ]
    for copy in started:
        copy.start()
    return started


def one_hot(index_tile, width):
    rows = index_tile.shape[0]
    padded = index_tile
    if rows < LANES:
        padded = jnp.concatenate(
            [index_tile, jnp.zeros((LANES - rows, LANES), index_tile.dtype)], axis=0
        )
    turned = jnp.transpose(padded)
    lane = lax.broadcasted_iota(jnp.int32, (LANES, width), 1).astype(jnp.float32)

    def make(row):
        return jnp.where(turned[:, row : row + 1] == lane, 1.0, 0.0).astype(jnp.bfloat16)

    return make


def send_setup(
    plan, own_h, slot_h, kind_h, normal_h, radii_h, rhs_h,
    message, mine, own, slot, kind, normal, radii, rhs, stack, sems,
):
    first = plan.near // LANES
    lanes = pl.ds(first * LANES, plan.contacts - first * LANES)
    for copy in fetch(
        [
            (own_h, own),
            (slot_h, slot),
            (kind_h, kind),
            (normal_h, normal),
            (radii_h.at[0, 0, 0, :, lanes], radii),
            (rhs_h, rhs),
        ],
        sems,
    ):
        copy.wait()
    for t in range(first, plan.tiles):
        at = (t - first) * 8
        lanes = slice(at * 16, at * 16 + LANES)
        stack[at : at + 1, :] = own[t : t + 1, :].astype(jnp.float32)
        stack[at + 1 : at + 2, :] = jnp.bitwise_and(slot[t : t + 1, :], plan.rim - 1).astype(
            jnp.float32
        )
        stack[at + 2 : at + 3, :] = kind[t : t + 1, :].astype(jnp.float32)
        stack[at + 3 : at + 6, :] = row_of(normal, t, plan.tiles, 3)
        stack[at + 6 : at + 8, :] = radii[:, lanes]
    lane = lax.broadcasted_iota(jnp.int32, (8, LANES), 1)
    row = lax.broadcasted_iota(jnp.int32, (8, LANES), 0)
    where = plan.neighbours()
    ghosts = [row_of(rhs, t, plan.grain_tiles, FIELDS) for t in range(plan.rim_tiles)]
    for e, (_, groups) in enumerate(plan.sides):
        chunk = jnp.where(row == 2, float(plan.types), 0.0)
        for j, k in enumerate(groups):
            place = plan.near + k * plan.group
            t, inside = place // LANES, place % LANES
            tile = stack[(t - first) * 8 : (t - first) * 8 + 8, :]
            turn = (j * plan.group - inside) % LANES
            if turn:
                tile = pltpu.roll(tile, turn, 1)
            here = (lane >= j * plan.group) & (lane < (j + 1) * plan.group)
            chunk = jnp.where(here, tile, chunk)
        mine[e * 8 : e * 8 + 8, :] = chunk
        packed = jnp.where(lane < plan.half, chunk, pltpu.roll(pltpu.roll(chunk, 4, 0), plan.half, 1))
        for t in range(plan.rim_tiles):
            message[where[e], 8 * t : 8 * t + FIELDS, :] = ghosts[t]
            message[where[e], 8 * t + FIELDS : 8 * t + 8, :] = packed[2 * t : 2 * t + 2, :]


def near_part(plan, field, diag, own, slot, table, hot, image, seen, push, left, queue=None):
    tiles = [field[:, s * LANES : (s + 1) * LANES] for s in range(plan.grain_tiles)]
    parts = plan.grains // plan.rim
    queue = queue or Queue()
    found = []
    for start, stop in plan.near_groups:
        rows = stop - start
        base = 2 * start
        for side, index in enumerate((own, slot)):
            for t in range(rows):
                at = (base + side * rows + t) * 8
                seen[at : at + 8, :] = lane_gather(tiles, spread(index, start + t))
                queue.run(1)
        one, two = base * 8, (base + rows) * 8
        first = [row_of(seen, one + c, 8, rows) for c in range(FIELDS)]
        second = [row_of(seen, two + c, 8, rows) for c in range(FIELDS)]
        consts = [table[k, start:stop, :] for k in range(9)]
        force, lever, moment = response(first, second, consts)
        zero = jnp.zeros((rows, LANES), jnp.float32)
        for c in range(3):
            push[pl.ds(one + c, rows, stride=8), :] = force[c]
            push[pl.ds(one + 3 + c, rows, stride=8), :] = consts[3] * lever[c] + moment[c]
            push[pl.ds(two + c, rows, stride=8), :] = -force[c]
            push[pl.ds(two + 3 + c, rows, stride=8), :] = consts[4] * lever[c] - moment[c]
        for c in range(FIELDS, 8):
            push[pl.ds(one + c, rows, stride=8), :] = zero
            push[pl.ds(two + c, rows, stride=8), :] = zero
        for side, index in enumerate((own, slot)):
            for t in range(rows):
                at = base + side * rows + t
                lanes = slice(at * LANES, (at + 1) * LANES)
                split = three_parts(push[at * 8 : at * 8 + 8, :])
                part = lax.shift_right_logical(spread(index, start + t), plan.rim_bits)
                lows = []
                for q in range(parts):
                    here = part == q
                    high, middle, low = [jnp.where(here, x, 0.0) for x in split]
                    left[q * 16 : q * 16 + 16, lanes] = stacked(high, middle)
                    lows.append(low)
                for q in range(0, parts, 2):
                    left[parts * 16 + q * 8 : parts * 16 + q * 8 + 16, lanes] = stacked(
                        lows[q], lows[q + 1]
                    )
        queue.add(left, hot, found, base * LANES, (base + 2 * rows) * LANES)
    queue.run()
    (total,) = found
    for q in range(parts):
        lanes = slice(q * plan.rim, (q + 1) * plan.rim)
        at = parts * 16 + q * 8
        force = total[at : at + 8, :] + total[q * 16 + 8 : q * 16 + 16, :]
        force = force + total[q * 16 : q * 16 + 8, :]
        image[:, lanes] = diag[:, lanes] * field[:, lanes] - force


def near_first(
    plan, stiff_h, own_h, slot_h, kind_h, normal_h, radii_h, rhs_h, diag_h,
    image, table, field, diag, own, slot, stiff, hot, kind, radii, rhs, ground, seen, push, left, sems,
):
    rows = plan.near_tiles
    copies = fetch(
        [
            (stiff_h, stiff),
            (own_h, own),
            (slot_h, slot),
            (kind_h, kind),
            (radii_h.at[0, 0, 0], radii),
            (rhs_h, rhs),
            (diag_h, ground),
        ]
        + [(normal_h.at[pl.ds(c * plan.tiles, plan.tiles), :], table.at[c]) for c in range(3)],
        sems,
    )
    for copy in copies:
        copy.wait()
    for source, target in ((rhs, field), (ground, diag)):
        target[FIELDS:, :] = jnp.zeros((8 - FIELDS, plan.grains), jnp.float32)
        for t in range(plan.grain_tiles):
            target[0:FIELDS, t * LANES : (t + 1) * LANES] = row_of(
                source, t, plan.grain_tiles, FIELDS
            )
    for t in range(rows):
        lanes = slice(t * LANES, (t + 1) * LANES)
        for c in range(2):
            table[3 + c, t : t + 1, :] = radii[c : c + 1, lanes]
    lane = lax.broadcasted_iota(jnp.int32, (rows, LANES), 1)
    line = lax.broadcasted_iota(jnp.int32, (rows, LANES), 0)
    valid = line * LANES + lane < plan.near
    for k, value in enumerate(coefficients(stiff, kind[0:rows, :], plan.types, valid)):
        table[5 + k, 0:rows, :] = value
    for side, index in enumerate((own, slot)):
        low = jnp.bitwise_and(index[...], plan.rim - 1).astype(jnp.float32)
        make = one_hot(low, plan.rim)
        for start, stop in plan.near_groups:
            for t in range(start, stop):
                at = (2 * start + side * (stop - start) + t - start) * LANES
                hot[at : at + LANES, :] = make(t)
    near_part(plan, field, diag, own, slot, table, hot, image, seen, push, left)


def far_push(plan, local, there, table, hot, push, left, queue):
    rows = plan.far
    first = [row_of(local, c, 8, rows) for c in range(FIELDS)]
    second = [row_of(there, c, 8, rows) for c in range(FIELDS)]
    consts = [table[k, 0:rows, :] for k in range(9)]
    force, lever, moment = response(first, second, consts)
    for c in range(3):
        push[pl.ds(c, rows, stride=8), :] = force[c]
        push[pl.ds(3 + c, rows, stride=8), :] = consts[3] * lever[c] + moment[c]
    zero = jnp.zeros((rows, LANES), jnp.float32)
    for c in range(FIELDS, 8):
        push[pl.ds(c, rows, stride=8), :] = zero
    for e in range(rows):
        lanes = slice(e * LANES, (e + 1) * LANES)
        high, middle, low = three_parts(push[e * 8 : e * 8 + 8, :])
        left[0:16, lanes] = stacked(high, middle)
        left[16:32, lanes] = stacked(low, jnp.zeros_like(low))
    found = []
    queue.add(left, hot, found, 0, rows * LANES)
    return found


def far_total(found):
    (total,) = found
    return total[0:8, :] + (total[8:16, :] + total[16:24, :])


def send_rim(plan, field, index, sums, message, local):
    row = lax.broadcasted_iota(jnp.int32, (8, LANES), 0)
    base = jnp.where(row == FIELDS, sums[0], jnp.where(row == FIELDS + 1, sums[1], 0.0))
    message[...] = jnp.broadcast_to(base[None], message.shape)
    tiles = [field[:, t * LANES : (t + 1) * LANES] for t in range(plan.rim_tiles)]
    where = plan.neighbours()
    for e in range(plan.far):
        tile = lane_gather(tiles, spread(index, e))
        local[e * 8 : e * 8 + 8, :] = tile
        message[where[e], :, :] = jnp.where(row < FIELDS, pltpu.roll(tile, plan.half, 1), base)


def partial_sums(r, w, s=None, p=None):
    def fold(product):
        total = product[:, 0:LANES]
        for t in range(1, product.shape[1] // LANES):
            total = total + product[:, t * LANES : (t + 1) * LANES]
        return total

    def join(left, right):
        low = lax.broadcasted_iota(jnp.int32, (8, LANES), 1) < LANES // 2
        halves = [x + pltpu.roll(x, LANES // 2, 1) for x in (left, right)]
        return jnp.sum(jnp.where(low, *halves), axis=0, keepdims=True)

    if s is None:
        zero = jnp.zeros((8, LANES), jnp.float32)
        return join(fold(r * r), zero), join(fold(w * r), zero)
    return join(fold(r * r), fold(r * s + p * w)), join(fold(w * r), fold(p * s))


def full_sums(received, first):
    low = lax.broadcasted_iota(jnp.int32, (1, LANES), 1) < LANES // 2
    found = []
    for row in (first, first + 1):
        total = jnp.sum(received[:, row, :], axis=0, keepdims=True)
        for half in (jnp.where(low, total, 0.0), jnp.where(low, 0.0, total)):
            found.append(jnp.sum(half, axis=1, keepdims=True))
    return found[0], found[2], found[1], found[3]


def step_sizes(sums, past):
    gamma, delta, mixed, energy = sums
    beta = gamma / past[0:1, 0:1]
    return gamma / (delta + beta * (mixed + beta * energy)), beta


def far_first(
    plan, stiff, received, mine, field, image,
    w, message, table, index, hot, local, merged, there, push, left,
):
    lane8 = lax.broadcasted_iota(jnp.int32, (8, LANES), 1)
    where = plan.neighbours()
    rows = plan.far
    for e in range(rows):
        own = pltpu.roll(mine[e * 8 : e * 8 + 8, :], plan.half, 1)
        packed = jnp.concatenate(
            [
                received[where[e], 8 * t + FIELDS : 8 * t + 8, :]
                for t in range(plan.rim_tiles)
            ],
            axis=0,
        )
        chunk = jnp.concatenate([packed, pltpu.roll(packed, plan.half, 1)], axis=0)
        merged[e * 8 : e * 8 + 8, :] = jnp.where(lane8 < plan.half, chunk, own)
    mirror = lax.broadcasted_iota(jnp.int32, (rows, LANES), 1) < plan.half
    row = [row_of(merged, r, 8, rows) for r in range(8)]
    for c in range(3):
        table[c, 0:rows, :] = jnp.where(mirror, -row[3 + c], row[3 + c])
    table[3, 0:rows, :] = jnp.where(mirror, row[7], row[6])
    table[4, 0:rows, :] = jnp.where(mirror, row[6], row[7])
    for k, value in enumerate(coefficients(stiff, row[2], plan.types)):
        table[5 + k, 0:rows, :] = value
    here = jnp.where(mirror, row[1], row[0])
    away = jnp.where(mirror, row[0], row[1]).astype(jnp.int32)
    index[0:rows, :] = here.astype(jnp.int32)
    make = one_hot(here, plan.rim)
    tiles = [field[:, t * LANES : (t + 1) * LANES] for t in range(plan.rim_tiles)]
    for e in range(rows):
        hot[e * LANES : (e + 1) * LANES, :] = make(e)
        local[e * 8 : e * 8 + 8, :] = lane_gather(tiles, spread(index, e))
        ghosts = [received[where[e], 8 * t : 8 * t + 8, :] for t in range(plan.rim_tiles)]
        there[e * 8 : e * 8 + 8, :] = lane_gather(
            ghosts, jnp.broadcast_to(away[e : e + 1, :], (8, LANES))
        )
    queue = Queue()
    found = far_push(plan, local, there, table, hot, push, left, queue)
    queue.run()
    force = far_total(found)
    w[...] = image[...]
    w[:, 0 : plan.rim] = image[:, 0 : plan.rim] - force
    sums = partial_sums(field[...], w[...])
    send_rim(plan, w, index, sums, message, local)


def far_step(plan, number, *refs):
    refs = list(refs)

    def take(count):
        return [refs.pop(0) for _ in range(count)]

    received, diag, own, slot, near_const, near_hot, table, index, hot, local, r, w = take(12)
    if number:
        p, s, z, x, past = take(5)
    last = number == ITERS - 2
    r_new, p_new, s_new, x_new, w_new, past_new = take(6)
    if not last:
        z_new, message, local_new = take(3)
    else:
        (message,) = take(1)
    image, near_seen, near_push, near_left, there, push, left = take(7)

    where = plan.neighbours()
    for e in range(plan.far):
        there[e * 8 : e * 8 + 8, :] = received[where[e], :, :]
    sums = full_sums(received, FIELDS)
    queue = Queue()
    found = far_push(plan, local, there, table, hot, push, left, queue)
    near_part(
        plan, w, diag, own, slot, near_const, near_hot, image, near_seen, near_push, near_left, queue
    )
    force = far_total(found)
    q = jnp.concatenate(
        [image[:, 0 : plan.rim] - force, image[:, plan.rim :]], axis=1
    )
    if number:
        alpha, beta = step_sizes(sums, past)
        z_now = q + beta * z[...]
        s_now = w[...] + beta * s[...]
        p_now = r[...] + beta * p[...]
        x_new[...] = x[...] + alpha * p_now
    else:
        alpha = sums[0] / sums[1]
        z_now = q
        s_now = w[...]
        p_now = r[...]
        x_new[...] = alpha * p_now
    r_now = r[...] - alpha * s_now
    w_now = w[...] - alpha * z_now
    r_new[...] = r_now
    w_new[...] = w_now
    p_new[...] = p_now
    s_new[...] = s_now
    past_new[...] = jnp.broadcast_to(sums[0], past_new.shape)
    sums = partial_sums(r_now, w_now, s_now, p_now)
    if not last:
        z_new[...] = z_now
        send_rim(plan, w_new, index, sums, message, local_new)
    else:
        base = jnp.concatenate(sums, axis=0)
        message[...] = jnp.broadcast_to(base[None], message.shape)


def finish(plan, received, r, w, p, s, x, past, x_out, r_out, x_last, r_last, sems):
    alpha, beta = step_sizes(full_sums(received, 0), past)
    for t in range(plan.grain_tiles):
        here = slice(0, FIELDS), slice(t * LANES, (t + 1) * LANES)
        there = pl.ds(t, FIELDS, stride=plan.grain_tiles), slice(None)
        x_last[there] = x[here] + alpha * (r[here] + beta * p[here])
        r_last[there] = r[here] - alpha * (w[here] + beta * s[here])
    for copy in fetch([(x_last, x_out), (r_last, r_out)], sems):
        copy.wait()


def shards(
    mesh,
    right_side,
    grain_diag,
    stiffness,
    contact_own,
    contact_slot,
    contact_type,
    contact_normal,
    contact_radii,
):
    plan = Plan(mesh, right_side.shape[-1], contact_own.shape[-1], stiffness.shape[1])
    own = contact_own.reshape(plan.tiles, LANES)
    slot = contact_slot.reshape(plan.tiles, LANES)
    kind = contact_type.reshape(plan.tiles, LANES)
    normal = contact_normal.reshape(3 * plan.tiles, LANES)
    lines = (FIELDS * plan.grain_tiles, LANES)
    rhs = right_side.reshape(lines)
    ground = grain_diag.reshape(lines)
    f32, bf16, i32 = jnp.float32, jnp.bfloat16, jnp.int32
    vmem, hbm, dma = pltpu.MemorySpace.VMEM, pltpu.MemorySpace.HBM, pltpu.SemaphoreType.DMA
    wide = (8, plan.grains)
    far = (plan.far * 8, LANES)
    far_table = (9, -(-plan.far // 8) * 8, LANES)
    near_table = (9, plan.tiles, LANES)
    table = (plan.tiles, LANES)
    near_rows = 2 * plan.near_tiles
    parts = plan.grains // plan.rim
    rest = plan.contacts - plan.near // LANES * LANES

    def call(body, outs, scratch, *args, raw=False, end=False):
        space = hbm if raw else vmem
        args = [pltpu.with_memory_space_constraint(x, space) for x in args]
        return pl.pallas_call(
            functools.partial(body, plan),
            out_shape=[(hbm if end else vmem)(dims, dtype) for dims, dtype in outs],
            in_specs=[pl.BlockSpec(memory_space=space)] * len(args),
            out_specs=[pl.BlockSpec(memory_space=hbm if end else vmem)] * len(outs),
            scratch_shapes=scratch,
            compiler_params=pltpu.CompilerParams(vmem_limit_bytes=16 * 2**20),
        )(*args)

    def exchange(message):
        return lax.all_to_all(message, AXES, 0, 0)

    tile = (plan.devices, 8, LANES)
    near_scratch = [
        vmem((near_rows * 8, LANES), f32),
        vmem((near_rows * 8, LANES), f32),
        vmem((parts * 24, near_rows * LANES), bf16),
    ]
    far_scratch = [vmem(far, f32), vmem(far, f32), vmem((32, plan.far * LANES), bf16)]

    message, mine = call(
        send_setup,
        [((plan.devices, 8 * plan.rim_tiles, LANES), f32), (far, f32)],
        [
            vmem(table, i32),
            vmem(table, i32),
            vmem(table, i32),
            vmem(normal.shape, f32),
            vmem((2, rest), f32),
            vmem(lines, f32),
            vmem((rest // LANES * 8, LANES), f32),
            dma((6,)),
        ],
        own, slot, kind, normal, contact_radii, rhs,
        raw=True,
    )
    received = exchange(message)
    image, near_const, field, diag, own, slot, stiff, near_hot = call(
        near_first,
        [
            (wide, f32),
            (near_table, f32),
            (wide, f32),
            (wide, f32),
            (table, i32),
            (table, i32),
            (stiffness.shape, f32),
            ((near_rows * LANES, plan.rim), bf16),
        ],
        [vmem(table, i32), vmem((2, plan.contacts), f32), vmem(lines, f32), vmem(lines, f32)]
        + near_scratch
        + [dma((10,))],
        stiffness, own, slot, kind, normal, contact_radii, rhs, ground,
        raw=True,
    )
    w, message, far_const, index, far_hot, local = call(
        far_first,
        [
            (wide, f32),
            (tile, f32),
            (far_table, f32),
            (far_table[1:], i32),
            ((plan.far * LANES, plan.rim), bf16),
            (far, f32),
        ],
        [vmem(far, f32)] + far_scratch,
        stiff, received, mine, field, image,
    )
    r = field
    state = ()
    for number in range(ITERS - 1):
        received = exchange(message)
        last = number == ITERS - 2
        outs = [(wide, f32)] * 5 + [((8, LANES), f32)]
        if last:
            outs = outs + [((plan.devices, 2, LANES), f32)]
        else:
            outs = outs + [(wide, f32), (tile, f32), (far, f32)]
        made = call(
            lambda plan, *refs, number=number: far_step(plan, number, *refs),
            outs,
            [vmem(wide, f32)] + near_scratch + far_scratch,
            received, diag, own, slot, near_const, near_hot, far_const, index, far_hot, local, r, w, *state,
        )
        r, p, s, x, w, past = made[:6]
        if last:
            message = made[6]
        else:
            z, message, local = made[6:]
            state = (p, s, z, x, past)
    received = exchange(message)
    solution_field, residual = call(
        finish,
        [(lines, f32)] * 2,
        [vmem(lines, f32), vmem(lines, f32), dma((2,))],
        received, r, w, p, s, x, past,
        end=True,
    )
    return (solution_field.reshape(right_side.shape), residual.reshape(right_side.shape))


def solution(mesh):
    vector = P("gx", "gy", "gz", None)
    matrix = P("gx", "gy", "gz", None, None)
    return jax.shard_map(
        functools.partial(shards, mesh),
        mesh=mesh,
        in_specs=(matrix, matrix, P(), vector, vector, vector, matrix, matrix),
        out_specs=(matrix, matrix),
        check_vma=False,
    )
```

```python
import functools

import jax
import jax.numpy as jnp
from jax import lax
from jax.experimental import pallas as pl
from jax.experimental.pallas import tpu as pltpu
from jax.sharding import PartitionSpec as P

ITERS = 4
AXES = ("gx", "gy", "gz")
LANES = 128
FIELDS = 6


class Plan:
    def __init__(self, mesh, grains, contacts, types):
        self.counts = tuple(mesh.shape[axis] for axis in AXES)
        self.devices = self.counts[0] * self.counts[1] * self.counts[2]
        self.grains = grains
        self.rim = grains // 4
        self.rim_bits = self.rim.bit_length() - 1
        self.group = grains // 32
        self.contacts = contacts
        self.types = types
        self.near = contacts - 26 * self.group
        self.near_tiles = -(-self.near // LANES)
        middle = self.near_tiles // 16 * 8
        self.near_groups = [(t, min(t + 8, self.near_tiles)) for t in range(0, self.near_tiles, 8)]
        self.tiles = contacts // LANES
        self.grain_tiles = grains // LANES
        self.rim_tiles = self.rim // LANES
        sides = {}
        for k in range(26):
            whole = k + (1 if k >= 13 else 0)
            offset = (whole // 9 - 1, whole // 3 % 3 - 1, whole % 3 - 1)
            delta = tuple(o % c for o, c in zip(offset, self.counts))
            sides.setdefault(delta, []).append(k)
        self.sides = sorted(sides.items())
        self.far = len(self.sides)
        most = max(len(groups) for groups in sides.values())
        self.half = -(-most * self.group // (LANES // 2)) * (LANES // 2)
        assert self.half * 2 == LANES and self.rim_tiles == 2 and self.counts[2] % 2 == 0

    def neighbours(self):
        place = [lax.axis_index(axis) for axis in AXES]
        found = []
        for delta, _ in self.sides:
            x, y, z = (lax.rem(p + d, c) for p, d, c in zip(place, delta, self.counts))
            found.append((x * self.counts[1] + y) * self.counts[2] + z)
        return found


def row_of(ref, row, stride, count):
    return ref[pl.ds(row, count, stride=stride), :]


def lane_gather(tiles, index):
    low = jnp.bitwise_and(index, LANES - 1)
    found = [jnp.take_along_axis(t, low, axis=1, mode="promise_in_bounds") for t in tiles]
    bit = LANES
    while len(found) > 1:
        odd = jnp.bitwise_and(index, bit) != 0
        found = [jnp.where(odd, b, a) for a, b in zip(found[0::2], found[1::2])]
        bit *= 2
    return found[0]


class Queue:
    def __init__(self):
        self.waiting = []

    def add(self, left, hot, sums, start, stop):
        step = 4 * LANES
        for at in range(start, stop, step):
            self.waiting.append((left, hot, sums, slice(at, min(at + step, stop))))

    def run(self, count=None):
        for _ in range(len(self.waiting) if count is None else min(count, len(self.waiting))):
            left, hot, sums, lanes = self.waiting.pop(0)
            sums.append(jnp.dot(left[:, lanes], hot[lanes, :], preferred_element_type=jnp.float32))
            if len(sums) == 2:
                sums[:] = [sums[0] + sums[1]]


def spread(ref, row):
    return jnp.broadcast_to(ref[row : row + 1, :], (8, LANES))


def coefficients(stiff_ref, kind, types, valid=None):
    found = []
    for which in range(4):
        total = jnp.zeros(kind.shape, jnp.float32)
        for t in range(types):
            total = jnp.where(kind == t, stiff_ref[which : which + 1, t : t + 1], total)
        if valid is not None:
            total = jnp.where(valid, total, 0.0)
        found.append(total)
    normal_k, shear_k, roll_k, twist_k = found
    return shear_k, normal_k - shear_k, roll_k, twist_k - roll_k


def response(first, second, table):
    n = table[0:3]
    first_r, second_r, shear_k, normal_d, roll_k, twist_d = table[3:]
    p = [second_r * second[3 + c] + first_r * first[3 + c] for c in range(3)]
    delta = []
    for c in range(3):
        a, b = (c + 1) % 3, (c + 2) % 3
        delta.append(second[c] - first[c] - (p[a] * n[b] - p[b] * n[a]))
    theta = [second[3 + c] - first[3 + c] for c in range(3)]
    along = normal_d * (n[0] * delta[0] + n[1] * delta[1] + n[2] * delta[2])
    twist = twist_d * (n[0] * theta[0] + n[1] * theta[1] + n[2] * theta[2])
    force = [shear_k * delta[c] + along * n[c] for c in range(3)]
    moment = [roll_k * theta[c] + twist * n[c] for c in range(3)]
    lever = []
    for c in range(3):
        a, b = (c + 1) % 3, (c + 2) % 3
        lever.append(n[a] * force[b] - n[b] * force[a])
    return force, lever, moment


def three_parts(value):
    high = value.astype(jnp.bfloat16).astype(jnp.float32)
    rest = value - high
    middle = rest.astype(jnp.bfloat16).astype(jnp.float32)
    return high, middle, rest - middle


def stacked(upper, lower):
    return jnp.concatenate([upper, lower], axis=0).astype(jnp.bfloat16)


def fetch(copies, sems):
    started = [
        pltpu.make_async_copy(source, target, sems.at[i])
        for i, (source, target) in enumerate(copies)
    ]
    for copy in started:
        copy.start()
    return started


def one_hot(index_tile, width):
    rows = index_tile.shape[0]
    padded = index_tile
    if rows < LANES:
        padded = jnp.concatenate(
            [index_tile, jnp.zeros((LANES - rows, LANES), index_tile.dtype)], axis=0
        )
    turned = jnp.transpose(padded)
    lane = lax.broadcasted_iota(jnp.int32, (LANES, width), 1).astype(jnp.float32)

    def make(row):
        return jnp.where(turned[:, row : row + 1] == lane, 1.0, 0.0).astype(jnp.bfloat16)

    return make


def send_setup(
    plan, own_h, slot_h, kind_h, normal_h, radii_h, rhs_h,
    message, mine, own, slot, kind, normal, radii, rhs, stack, sems,
):
    first = plan.near // LANES
    lanes = pl.ds(first * LANES, plan.contacts - first * LANES)
    for copy in fetch(
        [
            (own_h, own),
            (slot_h, slot),
            (kind_h, kind),
            (normal_h, normal.at[pl.ds(0, 3 * plan.tiles), :]),
            (radii_h.at[0, 0, 0, :, lanes], radii),
            (rhs_h, rhs.at[pl.ds(0, FIELDS * plan.grain_tiles), :]),
        ],
        sems,
    ):
        copy.wait()
    for t in range(first, plan.tiles):
        at = (t - first) * 8
        lanes = slice(at * 16, at * 16 + LANES)
        stack[at : at + 1, :] = own[t : t + 1, :].astype(jnp.float32)
        stack[at + 1 : at + 2, :] = jnp.bitwise_and(slot[t : t + 1, :], plan.rim - 1).astype(
            jnp.float32
        )
        stack[at + 2 : at + 3, :] = kind[t : t + 1, :].astype(jnp.float32)
        stack[at + 3 : at + 6, :] = row_of(normal, t, plan.tiles, 3)
        stack[at + 6 : at + 8, :] = radii[:, lanes]
    lane = lax.broadcasted_iota(jnp.int32, (8, LANES), 1)
    row = lax.broadcasted_iota(jnp.int32, (8, LANES), 0)
    where = plan.neighbours()
    ghosts = [row_of(rhs, t, plan.grain_tiles, FIELDS) for t in range(plan.rim_tiles)]
    for e, (_, groups) in enumerate(plan.sides):
        chunk = jnp.where(row == 2, float(plan.types), 0.0)
        for j, k in enumerate(groups):
            place = plan.near + k * plan.group
            t, inside = place // LANES, place % LANES
            tile = stack[(t - first) * 8 : (t - first) * 8 + 8, :]
            turn = (j * plan.group - inside) % LANES
            if turn:
                tile = pltpu.roll(tile, turn, 1)
            here = (lane >= j * plan.group) & (lane < (j + 1) * plan.group)
            chunk = jnp.where(here, tile, chunk)
        mine[e * 8 : e * 8 + 8, :] = chunk
        packed = jnp.where(lane < plan.half, chunk, pltpu.roll(pltpu.roll(chunk, 4, 0), plan.half, 1))
        for i in range(2):
            message[where[e], i, :, :] = packed[2 * i : 2 * i + 2, :]
    for d in range(plan.devices):
        for i in range(FIELDS // 2):
            message[d, 2 + i, :, :] = ghosts[d % 2][2 * i : 2 * i + 2, :]


def near_part(plan, field, diag, own, slot, table, hot, image, seen, push, left, queue=None):
    tiles = [field[:, s * LANES : (s + 1) * LANES] for s in range(plan.grain_tiles)]
    parts = plan.grains // plan.rim
    queue = queue or Queue()
    found = []
    for start, stop in plan.near_groups:
        rows = stop - start
        base = 2 * start
        for side, index in enumerate((own, slot)):
            for t in range(rows):
                at = (base + side * rows + t) * 8
                seen[at : at + 8, :] = lane_gather(tiles, spread(index, start + t))
                queue.run(1)
        one, two = base * 8, (base + rows) * 8
        first = [row_of(seen, one + c, 8, rows) for c in range(FIELDS)]
        second = [row_of(seen, two + c, 8, rows) for c in range(FIELDS)]
        consts = [table[k, start:stop, :] for k in range(9)]
        force, lever, moment = response(first, second, consts)
        zero = jnp.zeros((rows, LANES), jnp.float32)
        for c in range(3):
            push[pl.ds(one + c, rows, stride=8), :] = force[c]
            push[pl.ds(one + 3 + c, rows, stride=8), :] = consts[3] * lever[c] + moment[c]
            push[pl.ds(two + c, rows, stride=8), :] = -force[c]
            push[pl.ds(two + 3 + c, rows, stride=8), :] = consts[4] * lever[c] - moment[c]
        for c in range(FIELDS, 8):
            push[pl.ds(one + c, rows, stride=8), :] = zero
            push[pl.ds(two + c, rows, stride=8), :] = zero
        for side, index in enumerate((own, slot)):
            for t in range(rows):
                at = base + side * rows + t
                lanes = slice(at * LANES, (at + 1) * LANES)
                split = three_parts(push[at * 8 : at * 8 + 8, :])
                part = lax.shift_right_logical(spread(index, start + t), plan.rim_bits)
                lows = []
                for q in range(parts):
                    here = part == q
                    high, middle, low = [jnp.where(here, x, 0.0) for x in split]
                    left[q * 16 : q * 16 + 16, lanes] = stacked(high, middle)
                    lows.append(low)
                for q in range(0, parts, 2):
                    left[parts * 16 + q * 8 : parts * 16 + q * 8 + 16, lanes] = stacked(
                        lows[q], lows[q + 1]
                    )
        queue.add(left, hot, found, base * LANES, (base + 2 * rows) * LANES)
    queue.run()
    (total,) = found
    for q in range(parts):
        lanes = slice(q * plan.rim, (q + 1) * plan.rim)
        at = parts * 16 + q * 8
        force = total[at : at + 8, :] + total[q * 16 + 8 : q * 16 + 16, :]
        force = force + total[q * 16 : q * 16 + 8, :]
        image[:, lanes] = diag[:, lanes] * field[:, lanes] - force


def near_first(
    plan, stiff_h, own_h, slot_h, kind_h, normal_h, radii_h, rhs_h, diag_h,
    image, table, field, diag, own, slot, stiff, hot, kind, radii, rhs, ground, seen, push, left, sems,
):
    rows = plan.near_tiles
    lines = pl.ds(0, FIELDS * plan.grain_tiles)
    copies = fetch(
        [
            (stiff_h, stiff),
            (own_h, own),
            (slot_h, slot),
            (kind_h, kind),
            (radii_h.at[0, 0, 0], radii),
            (rhs_h, rhs.at[lines, :]),
            (diag_h, ground.at[lines, :]),
        ]
        + [(normal_h.at[pl.ds(c * plan.tiles, plan.tiles), :], table.at[c]) for c in range(3)],
        sems,
    )
    for copy in copies:
        copy.wait()
    for source, target in ((rhs, field), (ground, diag)):
        target[FIELDS:, :] = jnp.zeros((8 - FIELDS, plan.grains), jnp.float32)
        for t in range(plan.grain_tiles):
            target[0:FIELDS, t * LANES : (t + 1) * LANES] = row_of(
                source, t, plan.grain_tiles, FIELDS
            )
    for t in range(rows):
        lanes = slice(t * LANES, (t + 1) * LANES)
        for c in range(2):
            table[3 + c, t : t + 1, :] = radii[c : c + 1, lanes]
    lane = lax.broadcasted_iota(jnp.int32, (rows, LANES), 1)
    line = lax.broadcasted_iota(jnp.int32, (rows, LANES), 0)
    valid = line * LANES + lane < plan.near
    for k, value in enumerate(coefficients(stiff, kind[0:rows, :], plan.types, valid)):
        table[5 + k, 0:rows, :] = value
    for side, index in enumerate((own, slot)):
        low = jnp.bitwise_and(index[...], plan.rim - 1).astype(jnp.float32)
        make = one_hot(low, plan.rim)
        for start, stop in plan.near_groups:
            for t in range(start, stop):
                at = (2 * start + side * (stop - start) + t - start) * LANES
                hot[at : at + LANES, :] = make(t)
    near_part(plan, field, diag, own, slot, table, hot, image, seen, push, left)


def far_push(plan, local, there, table, hot, push, left, queue):
    rows = plan.far
    first = [row_of(local, c, 8, rows) for c in range(FIELDS)]
    second = [row_of(there, c, 8, rows) for c in range(FIELDS)]
    consts = [table[k, 0:rows, :] for k in range(9)]
    force, lever, moment = response(first, second, consts)
    for c in range(3):
        push[pl.ds(c, rows, stride=8), :] = force[c]
        push[pl.ds(3 + c, rows, stride=8), :] = consts[3] * lever[c] + moment[c]
    zero = jnp.zeros((rows, LANES), jnp.float32)
    for c in range(FIELDS, 8):
        push[pl.ds(c, rows, stride=8), :] = zero
    for e in range(rows):
        lanes = slice(e * LANES, (e + 1) * LANES)
        high, middle, low = three_parts(push[e * 8 : e * 8 + 8, :])
        left[0:16, lanes] = stacked(high, middle)
        left[16:32, lanes] = stacked(low, jnp.zeros_like(low))
    found = []
    queue.add(left, hot, found, 0, rows * LANES)
    return found


def far_total(found):
    (total,) = found
    return total[0:8, :] + (total[8:16, :] + total[16:24, :])


def send_rim(plan, field, index, sums, message, local):
    row = lax.broadcasted_iota(jnp.int32, (8, LANES), 0)
    base = jnp.where(row == FIELDS, sums[0], jnp.where(row == FIELDS + 1, sums[1], 0.0))
    message[...] = jnp.broadcast_to(base[None], message.shape)
    tiles = [field[:, t * LANES : (t + 1) * LANES] for t in range(plan.rim_tiles)]
    where = plan.neighbours()
    for e in range(plan.far):
        tile = lane_gather(tiles, spread(index, e))
        local[e * 8 : e * 8 + 8, :] = tile
        message[where[e], :, :] = jnp.where(row < FIELDS, pltpu.roll(tile, plan.half, 1), base)


def partial_sums(r, w, s=None, p=None):
    def fold(product):
        total = product[:, 0:LANES]
        for t in range(1, product.shape[1] // LANES):
            total = total + product[:, t * LANES : (t + 1) * LANES]
        return total

    def join(left, right):
        low = lax.broadcasted_iota(jnp.int32, (8, LANES), 1) < LANES // 2
        halves = [x + pltpu.roll(x, LANES // 2, 1) for x in (left, right)]
        return jnp.sum(jnp.where(low, *halves), axis=0, keepdims=True)

    if s is None:
        zero = jnp.zeros((8, LANES), jnp.float32)
        return join(fold(r * r), zero), join(fold(w * r), zero)
    return join(fold(r * r), fold(r * s + p * w)), join(fold(w * r), fold(p * s))


def full_sums(received, first):
    low = lax.broadcasted_iota(jnp.int32, (1, LANES), 1) < LANES // 2
    found = []
    for row in (first, first + 1):
        total = jnp.sum(received[:, row, :], axis=0, keepdims=True)
        for half in (jnp.where(low, total, 0.0), jnp.where(low, 0.0, total)):
            found.append(jnp.sum(half, axis=1, keepdims=True))
    return found[0], found[2], found[1], found[3]


def step_sizes(sums, past):
    gamma, delta, mixed, energy = sums
    beta = gamma / past[0:1, 0:1]
    return gamma / (delta + beta * (mixed + beta * energy)), beta


def far_tables(
    plan, stiff, received, mine, field, table, index, away, hot, local, merged,
):
    lane8 = lax.broadcasted_iota(jnp.int32, (8, LANES), 1)
    where = plan.neighbours()
    rows = plan.far
    for e in range(rows):
        own = pltpu.roll(mine[e * 8 : e * 8 + 8, :], plan.half, 1)
        packed = jnp.concatenate([received[where[e], 0], received[where[e], 1]], axis=0)
        chunk = jnp.concatenate([packed, pltpu.roll(packed, plan.half, 1)], axis=0)
        merged[e * 8 : e * 8 + 8, :] = jnp.where(lane8 < plan.half, chunk, own)
    mirror = lax.broadcasted_iota(jnp.int32, (rows, LANES), 1) < plan.half
    row = [row_of(merged, r, 8, rows) for r in range(8)]
    for c in range(3):
        table[c, 0:rows, :] = jnp.where(mirror, -row[3 + c], row[3 + c])
    table[3, 0:rows, :] = jnp.where(mirror, row[7], row[6])
    table[4, 0:rows, :] = jnp.where(mirror, row[6], row[7])
    for k, value in enumerate(coefficients(stiff, row[2], plan.types)):
        table[5 + k, 0:rows, :] = value
    here = jnp.where(mirror, row[1], row[0])
    index[0:rows, :] = here.astype(jnp.int32)
    away[0:rows, :] = jnp.where(mirror, row[0], row[1]).astype(jnp.int32)
    make = one_hot(here, plan.rim)
    tiles = [field[:, t * LANES : (t + 1) * LANES] for t in range(plan.rim_tiles)]
    for e in range(rows):
        hot[e * LANES : (e + 1) * LANES, :] = make(e)
        local[e * 8 : e * 8 + 8, :] = lane_gather(tiles, spread(index, e))


def far_first(
    plan, received, swapped, table, index, away, hot, local, field, image,
    w, message, local_new, there, push, left,
):
    where = plan.neighbours()
    half = lax.rem(lax.axis_index(AXES[2]), 2)
    for e in range(plan.far):
        wanted = spread(away, e)
        low = jnp.bitwise_and(wanted, LANES - 1)
        found = []
        for source in (received, swapped):
            rows = [source[where[e], 2 + i] for i in (0, 1, 2, 2)]
            tile = jnp.concatenate(rows, axis=0)
            found.append(jnp.take_along_axis(tile, low, axis=1, mode="promise_in_bounds"))
        there[e * 8 : e * 8 + 8, :] = jnp.where(
            lax.shift_right_logical(wanted, 7) == half, found[0], found[1]
        )
    queue = Queue()
    found = far_push(plan, local, there, table, hot, push, left, queue)
    queue.run()
    force = far_total(found)
    w[...] = image[...]
    w[:, 0 : plan.rim] = image[:, 0 : plan.rim] - force
    sums = partial_sums(field[...], w[...])
    send_rim(plan, w, index, sums, message, local_new)


def far_step(plan, number, *refs):
    refs = list(refs)

    def take(count):
        return [refs.pop(0) for _ in range(count)]

    received, diag, own, slot, near_const, near_hot, table, index, hot, local, r, w = take(12)
    if number:
        p, s, z, x, past = take(5)
    last = number == ITERS - 2
    r_new, p_new, s_new, x_new, w_new, past_new = take(6)
    if not last:
        z_new, message, local_new = take(3)
    else:
        (message,) = take(1)
    image, near_seen, near_push, near_left, there, push, left = take(7)

    where = plan.neighbours()
    for e in range(plan.far):
        there[e * 8 : e * 8 + 8, :] = received[where[e], :, :]
    sums = full_sums(received, FIELDS)
    queue = Queue()
    found = far_push(plan, local, there, table, hot, push, left, queue)
    near_part(
        plan, w, diag, own, slot, near_const, near_hot, image, near_seen, near_push, near_left, queue
    )
    force = far_total(found)
    q = jnp.concatenate(
        [image[:, 0 : plan.rim] - force, image[:, plan.rim :]], axis=1
    )
    if number:
        alpha, beta = step_sizes(sums, past)
        z_now = q + beta * z[...]
        s_now = w[...] + beta * s[...]
        p_now = r[...] + beta * p[...]
        x_new[...] = x[...] + alpha * p_now
    else:
        alpha = sums[0] / sums[1]
        z_now = q
        s_now = w[...]
        p_now = r[...]
        x_new[...] = alpha * p_now
    r_now = r[...] - alpha * s_now
    w_now = w[...] - alpha * z_now
    r_new[...] = r_now
    w_new[...] = w_now
    p_new[...] = p_now
    s_new[...] = s_now
    past_new[...] = jnp.broadcast_to(sums[0], past_new.shape)
    sums = partial_sums(r_now, w_now, s_now, p_now)
    if not last:
        z_new[...] = z_now
        send_rim(plan, w_new, index, sums, message, local_new)
    else:
        base = jnp.concatenate(sums, axis=0)
        message[...] = jnp.broadcast_to(base[None], message.shape)


def finish(plan, received, r, w, p, s, x, past, x_out, r_out, x_last, r_last, sems):
    alpha, beta = step_sizes(full_sums(received, 0), past)
    for t in range(plan.grain_tiles):
        here = slice(0, FIELDS), slice(t * LANES, (t + 1) * LANES)
        there = pl.ds(t, FIELDS, stride=plan.grain_tiles), slice(None)
        x_last[there] = x[here] + alpha * (r[here] + beta * p[here])
        r_last[there] = r[here] - alpha * (w[here] + beta * s[here])
    lines = pl.ds(0, FIELDS * plan.grain_tiles)
    for copy in fetch([(x_last.at[lines, :], x_out), (r_last.at[lines, :], r_out)], sems):
        copy.wait()


def shards(
    mesh,
    right_side,
    grain_diag,
    stiffness,
    contact_own,
    contact_slot,
    contact_type,
    contact_normal,
    contact_radii,
):
    plan = Plan(mesh, right_side.shape[-1], contact_own.shape[-1], stiffness.shape[1])
    own = contact_own.reshape(plan.tiles, LANES)
    slot = contact_slot.reshape(plan.tiles, LANES)
    kind = contact_type.reshape(plan.tiles, LANES)
    normal = contact_normal.reshape(3 * plan.tiles, LANES)
    lines = (FIELDS * plan.grain_tiles, LANES)
    more_lines = (8 * plan.grain_tiles, LANES)
    rhs = right_side.reshape(lines)
    ground = grain_diag.reshape(lines)
    f32, bf16, i32 = jnp.float32, jnp.bfloat16, jnp.int32
    vmem, hbm, dma = pltpu.MemorySpace.VMEM, pltpu.MemorySpace.HBM, pltpu.SemaphoreType.DMA
    wide = (8, plan.grains)
    far = (-(-plan.far // 8) * 64, LANES)
    far_table = (9, -(-plan.far // 8) * 8, LANES)
    near_table = (9, plan.tiles, LANES)
    table = (plan.tiles, LANES)
    near_rows = 2 * plan.near_tiles
    parts = plan.grains // plan.rim
    rest = plan.contacts - plan.near // LANES * LANES

    def call(body, outs, scratch, *args, raw=False, end=False):
        space = hbm if raw else vmem
        args = [pltpu.with_memory_space_constraint(x, space) for x in args]
        return pl.pallas_call(
            functools.partial(body, plan),
            out_shape=[(hbm if end else vmem)(dims, dtype) for dims, dtype in outs],
            in_specs=[pl.BlockSpec(memory_space=space)] * len(args),
            out_specs=[pl.BlockSpec(memory_space=hbm if end else vmem)] * len(outs),
            scratch_shapes=scratch,
            compiler_params=pltpu.CompilerParams(vmem_limit_bytes=16 * 2**20),
        )(*args)

    def exchange(message):
        return lax.all_to_all(message, AXES, 0, 0)

    tile = (plan.devices, 8, LANES)
    near_scratch = [
        vmem((near_rows * 8 + 64, LANES), f32),
        vmem((near_rows * 8 + 64, LANES), f32),
        vmem((parts * 24, near_rows * LANES), bf16),
    ]
    far_scratch = [vmem(far, f32), vmem(far, f32), vmem((32, plan.far * LANES), bf16)]

    message, mine = call(
        send_setup,
        [((plan.devices, 2 + FIELDS // 2, 2, LANES), f32), (far, f32)],
        [
            vmem(table, i32),
            vmem(table, i32),
            vmem(table, i32),
            vmem((8 * plan.tiles, LANES), f32),
            vmem((2, rest), f32),
            vmem(more_lines, f32),
            vmem((rest // LANES * 8, LANES), f32),
            dma((6,)),
        ],
        own, slot, kind, normal, contact_radii, rhs,
        raw=True,
    )
    received = exchange(message)
    image, near_const, field, diag, own, slot, stiff, near_hot = call(
        near_first,
        [
            (wide, f32),
            (near_table, f32),
            (wide, f32),
            (wide, f32),
            (table, i32),
            (table, i32),
            (stiffness.shape, f32),
            ((near_rows * LANES, plan.rim), bf16),
        ],
        [vmem(table, i32), vmem((2, plan.contacts), f32), vmem(more_lines, f32), vmem(more_lines, f32)]
        + near_scratch
        + [dma((10,))],
        stiffness, own, slot, kind, normal, contact_radii, rhs, ground,
        raw=True,
    )
    pairs = [(i, i ^ 1) for i in range(plan.counts[2])]
    received, image = lax.optimization_barrier((received, image))
    swapped = lax.ppermute(received, AXES[2], pairs)
    far_const, index, away, far_hot, local = call(
        far_tables,
        [
            (far_table, f32),
            (far_table[1:], i32),
            (far_table[1:], i32),
            ((plan.far * LANES, plan.rim), bf16),
            (far, f32),
        ],
        [vmem(far, f32)],
        stiff, received, mine, field,
    )
    w, message, local = call(
        far_first,
        [(wide, f32), (tile, f32), (far, f32)],
        far_scratch,
        received, swapped, far_const, index, away, far_hot, local, field, image,
    )
    r = field
    state = ()
    for number in range(ITERS - 1):
        received = exchange(message)
        last = number == ITERS - 2
        outs = [(wide, f32)] * 5 + [((8, LANES), f32)]
        if last:
            outs = outs + [((plan.devices, 2, LANES), f32)]
        else:
            outs = outs + [(wide, f32), (tile, f32), (far, f32)]
        made = call(
            lambda plan, *refs, number=number: far_step(plan, number, *refs),
            outs,
            [vmem(wide, f32)] + near_scratch + far_scratch,
            received, diag, own, slot, near_const, near_hot, far_const, index, far_hot, local, r, w, *state,
        )
        r, p, s, x, w, past = made[:6]
        if last:
            message = made[6]
        else:
            z, message, local = made[6:]
            state = (p, s, z, x, past)
    received = exchange(message)
    solution_field, residual = call(
        finish,
        [(lines, f32)] * 2,
        [vmem(more_lines, f32), vmem(more_lines, f32), dma((2,))],
        received, r, w, p, s, x, past,
        end=True,
    )
    return (solution_field.reshape(right_side.shape), residual.reshape(right_side.shape))


def solution(mesh):
    vector = P("gx", "gy", "gz", None)
    matrix = P("gx", "gy", "gz", None, None)
    return jax.shard_map(
        functools.partial(shards, mesh),
        mesh=mesh,
        in_specs=(matrix, matrix, P(), vector, vector, vector, matrix, matrix),
        out_specs=(matrix, matrix),
        check_vma=False,
    )
```

```python
import functools

import jax
import jax.numpy as jnp
from jax import lax
from jax.experimental import pallas as pl
from jax.experimental.pallas import tpu as pltpu
from jax.sharding import PartitionSpec as P

ITERS = 4
AXES = ("gx", "gy", "gz")
LANES = 128
FIELDS = 6


class Plan:
    def __init__(self, mesh, grains, contacts, types):
        self.counts = tuple(mesh.shape[axis] for axis in AXES)
        self.devices = self.counts[0] * self.counts[1] * self.counts[2]
        self.grains = grains
        self.rim = grains // 4
        self.rim_bits = self.rim.bit_length() - 1
        self.group = grains // 32
        self.contacts = contacts
        self.types = types
        self.near = contacts - 26 * self.group
        self.near_tiles = -(-self.near // LANES)
        middle = self.near_tiles // 16 * 8
        self.near_groups = [(t, min(t + 8, self.near_tiles)) for t in range(0, self.near_tiles, 8)]
        self.tiles = contacts // LANES
        self.grain_tiles = grains // LANES
        self.rim_tiles = self.rim // LANES
        sides = {}
        for k in range(26):
            whole = k + (1 if k >= 13 else 0)
            offset = (whole // 9 - 1, whole // 3 % 3 - 1, whole % 3 - 1)
            delta = tuple(o % c for o, c in zip(offset, self.counts))
            sides.setdefault(delta, []).append(k)
        self.sides = sorted(sides.items())
        self.far = len(self.sides)
        most = max(len(groups) for groups in sides.values())
        self.half = -(-most * self.group // (LANES // 2)) * (LANES // 2)
        assert self.half * 2 == LANES and self.rim_tiles == 2 and self.counts[2] % 2 == 0

    def neighbours(self):
        place = [lax.axis_index(axis) for axis in AXES]
        found = []
        for delta, _ in self.sides:
            x, y, z = (lax.rem(p + d, c) for p, d, c in zip(place, delta, self.counts))
            found.append((x * self.counts[1] + y) * self.counts[2] + z)
        return found


def row_of(ref, row, stride, count):
    return ref[pl.ds(row, count, stride=stride), :]


def lane_gather(tiles, index):
    low = jnp.bitwise_and(index, LANES - 1)
    found = [jnp.take_along_axis(t, low, axis=1, mode="promise_in_bounds") for t in tiles]
    bit = LANES
    while len(found) > 1:
        odd = jnp.bitwise_and(index, bit) != 0
        found = [jnp.where(odd, b, a) for a, b in zip(found[0::2], found[1::2])]
        bit *= 2
    return found[0]


class Queue:
    def __init__(self):
        self.waiting = []

    def add(self, left, hot, sums, start, stop):
        step = 8 * LANES
        for at in range(start, stop, step):
            self.waiting.append((left, hot, sums, slice(at, min(at + step, stop))))

    def run(self, count=None):
        for _ in range(len(self.waiting) if count is None else min(count, len(self.waiting))):
            left, hot, sums, lanes = self.waiting.pop(0)
            sums.append(jnp.dot(left[:, lanes], hot[lanes, :], preferred_element_type=jnp.float32))
            if len(sums) == 2:
                sums[:] = [sums[0] + sums[1]]


def spread(ref, row):
    return jnp.broadcast_to(ref[row : row + 1, :], (8, LANES))


def coefficients(stiff_ref, kind, types, valid=None):
    found = []
    for which in range(4):
        total = jnp.zeros(kind.shape, jnp.float32)
        for t in range(types):
            total = jnp.where(kind == t, stiff_ref[which : which + 1, t : t + 1], total)
        if valid is not None:
            total = jnp.where(valid, total, 0.0)
        found.append(total)
    normal_k, shear_k, roll_k, twist_k = found
    return shear_k, normal_k - shear_k, roll_k, twist_k - roll_k


def response(first, second, table):
    n = table[0:3]
    first_r, second_r, shear_k, normal_d, roll_k, twist_d = table[3:]
    p = [second_r * second[3 + c] + first_r * first[3 + c] for c in range(3)]
    delta = []
    for c in range(3):
        a, b = (c + 1) % 3, (c + 2) % 3
        delta.append(second[c] - first[c] - (p[a] * n[b] - p[b] * n[a]))
    theta = [second[3 + c] - first[3 + c] for c in range(3)]
    along = normal_d * (n[0] * delta[0] + n[1] * delta[1] + n[2] * delta[2])
    twist = twist_d * (n[0] * theta[0] + n[1] * theta[1] + n[2] * theta[2])
    force = [shear_k * delta[c] + along * n[c] for c in range(3)]
    moment = [roll_k * theta[c] + twist * n[c] for c in range(3)]
    lever = []
    for c in range(3):
        a, b = (c + 1) % 3, (c + 2) % 3
        lever.append(n[a] * force[b] - n[b] * force[a])
    return force, lever, moment


def three_parts(value):
    high = value.astype(jnp.bfloat16).astype(jnp.float32)
    rest = value - high
    middle = rest.astype(jnp.bfloat16).astype(jnp.float32)
    return high, middle, rest - middle


def stacked(upper, lower):
    return jnp.concatenate([upper, lower], axis=0).astype(jnp.bfloat16)


def fetch(copies, sems):
    started = [
        pltpu.make_async_copy(source, target, sems.at[i])
        for i, (source, target) in enumerate(copies)
    ]
    for copy in started:
        copy.start()
    return started


def one_hot(index_tile, width):
    rows = index_tile.shape[0]
    padded = index_tile
    if rows < LANES:
        padded = jnp.concatenate(
            [index_tile, jnp.zeros((LANES - rows, LANES), index_tile.dtype)], axis=0
        )
    turned = jnp.transpose(padded)
    lane = lax.broadcasted_iota(jnp.int32, (LANES, width), 1).astype(jnp.float32)

    def make(row):
        return jnp.where(turned[:, row : row + 1] == lane, 1.0, 0.0).astype(jnp.bfloat16)

    return make


def send_setup(
    plan, own_h, slot_h, kind_h, normal_h, radii_h, rhs_h,
    message, mine, own, slot, kind, normal, radii, rhs, stack, sems,
):
    first = plan.near // LANES
    lanes = pl.ds(first * LANES, plan.contacts - first * LANES)
    for copy in fetch(
        [
            (own_h, own),
            (slot_h, slot),
            (kind_h, kind),
            (normal_h, normal.at[pl.ds(0, 3 * plan.tiles), :]),
            (radii_h.at[0, 0, 0, :, lanes], radii),
            (rhs_h, rhs.at[pl.ds(0, FIELDS * plan.grain_tiles), :]),
        ],
        sems,
    ):
        copy.wait()
    for t in range(first, plan.tiles):
        at = (t - first) * 8
        lanes = slice(at * 16, at * 16 + LANES)
        stack[at : at + 1, :] = own[t : t + 1, :].astype(jnp.float32)
        stack[at + 1 : at + 2, :] = jnp.bitwise_and(slot[t : t + 1, :], plan.rim - 1).astype(
            jnp.float32
        )
        stack[at + 2 : at + 3, :] = kind[t : t + 1, :].astype(jnp.float32)
        stack[at + 3 : at + 6, :] = row_of(normal, t, plan.tiles, 3)
        stack[at + 6 : at + 8, :] = radii[:, lanes]
    lane = lax.broadcasted_iota(jnp.int32, (8, LANES), 1)
    row = lax.broadcasted_iota(jnp.int32, (8, LANES), 0)
    where = plan.neighbours()
    ghosts = [row_of(rhs, t, plan.grain_tiles, FIELDS) for t in range(plan.rim_tiles)]
    for e, (_, groups) in enumerate(plan.sides):
        chunk = jnp.where(row == 2, float(plan.types), 0.0)
        for j, k in enumerate(groups):
            place = plan.near + k * plan.group
            t, inside = place // LANES, place % LANES
            tile = stack[(t - first) * 8 : (t - first) * 8 + 8, :]
            turn = (j * plan.group - inside) % LANES
            if turn:
                tile = pltpu.roll(tile, turn, 1)
            here = (lane >= j * plan.group) & (lane < (j + 1) * plan.group)
            chunk = jnp.where(here, tile, chunk)
        mine[e * 8 : e * 8 + 8, :] = chunk
        packed = jnp.where(lane < plan.half, chunk, pltpu.roll(pltpu.roll(chunk, 4, 0), plan.half, 1))
        for i in range(2):
            message[where[e], i, :, :] = packed[2 * i : 2 * i + 2, :]
    for d in range(plan.devices):
        for i in range(FIELDS // 2):
            message[d, 2 + i, :, :] = ghosts[d % 2][2 * i : 2 * i + 2, :]


def near_part(plan, field, diag, own, slot, table, hot, image, seen, push, left, queue=None, then=None):
    tiles = [field[:, s * LANES : (s + 1) * LANES] for s in range(plan.grain_tiles)]
    parts = plan.grains // plan.rim
    queue = queue or Queue()
    found = []
    for start, stop in plan.near_groups:
        rows = stop - start
        base = 2 * start
        for side, index in enumerate((own, slot)):
            for t in range(rows):
                at = (base + side * rows + t) * 8
                seen[at : at + 8, :] = lane_gather(tiles, spread(index, start + t))
                queue.run(1)
        if then and start == 0:
            then()
        one, two = base * 8, (base + rows) * 8
        first = [row_of(seen, one + c, 8, rows) for c in range(FIELDS)]
        second = [row_of(seen, two + c, 8, rows) for c in range(FIELDS)]
        consts = [table[k, start:stop, :] for k in range(9)]
        force, lever, moment = response(first, second, consts)
        zero = jnp.zeros((rows, LANES), jnp.float32)
        for c in range(3):
            push[pl.ds(one + c, rows, stride=8), :] = force[c]
            push[pl.ds(one + 3 + c, rows, stride=8), :] = consts[3] * lever[c] + moment[c]
            push[pl.ds(two + c, rows, stride=8), :] = -force[c]
            push[pl.ds(two + 3 + c, rows, stride=8), :] = consts[4] * lever[c] - moment[c]
        for c in range(FIELDS, 8):
            push[pl.ds(one + c, rows, stride=8), :] = zero
            push[pl.ds(two + c, rows, stride=8), :] = zero
        for side, index in enumerate((own, slot)):
            for t in range(rows):
                at = base + side * rows + t
                lanes = slice(at * LANES, (at + 1) * LANES)
                split = three_parts(push[at * 8 : at * 8 + 8, :])
                part = lax.shift_right_logical(spread(index, start + t), plan.rim_bits)
                lows = []
                pair = stacked(split[0], split[1])
                for q in range(parts):
                    here = jnp.where(part == q, 1.0, 0.0)
                    left[q * 16 : q * 16 + 16, lanes] = pair * stacked(here, here)
                    lows.append(split[2] * here)
                for q in range(0, parts, 2):
                    left[parts * 16 + q * 8 : parts * 16 + q * 8 + 16, lanes] = stacked(
                        lows[q], lows[q + 1]
                    )
        queue.add(left, hot, found, base * LANES, (base + 2 * rows) * LANES)
    queue.run()
    (total,) = found
    for q in range(parts):
        lanes = slice(q * plan.rim, (q + 1) * plan.rim)
        at = parts * 16 + q * 8
        force = total[at : at + 8, :] + total[q * 16 + 8 : q * 16 + 16, :]
        force = force + total[q * 16 : q * 16 + 8, :]
        image[:, lanes] = diag[:, lanes] * field[:, lanes] - force


def near_first(
    plan, stiff_h, own_h, slot_h, kind_h, normal_h, radii_h, rhs_h, diag_h,
    image, table, field, diag, own, slot, stiff, hot, kind, radii, rhs, ground, seen, push, left, sems,
):
    rows = plan.near_tiles
    lines = pl.ds(0, FIELDS * plan.grain_tiles)
    copies = fetch(
        [
            (stiff_h, stiff),
            (own_h, own),
            (slot_h, slot),
            (kind_h, kind),
            (radii_h.at[0, 0, 0], radii),
            (rhs_h, rhs.at[lines, :]),
            (diag_h, ground.at[lines, :]),
        ]
        + [(normal_h.at[pl.ds(c * plan.tiles, plan.tiles), :], table.at[c]) for c in range(3)],
        sems,
    )
    for copy in copies:
        copy.wait()
    for source, target in ((rhs, field), (ground, diag)):
        target[FIELDS:, :] = jnp.zeros((8 - FIELDS, plan.grains), jnp.float32)
        for t in range(plan.grain_tiles):
            target[0:FIELDS, t * LANES : (t + 1) * LANES] = row_of(
                source, t, plan.grain_tiles, FIELDS
            )
    for t in range(rows):
        lanes = slice(t * LANES, (t + 1) * LANES)
        for c in range(2):
            table[3 + c, t : t + 1, :] = radii[c : c + 1, lanes]
    lane = lax.broadcasted_iota(jnp.int32, (rows, LANES), 1)
    line = lax.broadcasted_iota(jnp.int32, (rows, LANES), 0)
    valid = line * LANES + lane < plan.near
    for k, value in enumerate(coefficients(stiff, kind[0:rows, :], plan.types, valid)):
        table[5 + k, 0:rows, :] = value
    for side, index in enumerate((own, slot)):
        low = jnp.bitwise_and(index[...], plan.rim - 1).astype(jnp.float32)
        make = one_hot(low, plan.rim)
        for start, stop in plan.near_groups:
            for t in range(start, stop):
                at = (2 * start + side * (stop - start) + t - start) * LANES
                hot[at : at + LANES, :] = make(t)
    near_part(plan, field, diag, own, slot, table, hot, image, seen, push, left)


def far_push(plan, local, there, table, hot, push, left, queue):
    rows = plan.far
    first = [row_of(local, c, 8, rows) for c in range(FIELDS)]
    second = [row_of(there, c, 8, rows) for c in range(FIELDS)]
    consts = [table[k, 0:rows, :] for k in range(9)]
    force, lever, moment = response(first, second, consts)
    for c in range(3):
        push[pl.ds(c, rows, stride=8), :] = force[c]
        push[pl.ds(3 + c, rows, stride=8), :] = consts[3] * lever[c] + moment[c]
    zero = jnp.zeros((rows, LANES), jnp.float32)
    for c in range(FIELDS, 8):
        push[pl.ds(c, rows, stride=8), :] = zero
    for e in range(rows):
        lanes = slice(e * LANES, (e + 1) * LANES)
        high, middle, low = three_parts(push[e * 8 : e * 8 + 8, :])
        left[0:16, lanes] = stacked(high, middle)
        left[16:32, lanes] = stacked(low, jnp.zeros_like(low))
    found = []
    queue.add(left, hot, found, 0, rows * LANES)
    return found


def far_total(found):
    (total,) = found
    return total[0:8, :] + (total[8:16, :] + total[16:24, :])


def send_rim(plan, field, index, sums, message, local):
    row = lax.broadcasted_iota(jnp.int32, (8, LANES), 0)
    base = jnp.where(row == FIELDS, sums[0], jnp.where(row == FIELDS + 1, sums[1], 0.0))
    message[...] = jnp.broadcast_to(base[None], message.shape)
    tiles = [field[:, t * LANES : (t + 1) * LANES] for t in range(plan.rim_tiles)]
    where = plan.neighbours()
    for e in range(plan.far):
        tile = lane_gather(tiles, spread(index, e))
        local[e * 8 : e * 8 + 8, :] = tile
        message[where[e], :, :] = jnp.where(row < FIELDS, pltpu.roll(tile, plan.half, 1), base)


def partial_sums(r, w, s=None, p=None):
    def fold(product):
        total = product[:, 0:LANES]
        for t in range(1, product.shape[1] // LANES):
            total = total + product[:, t * LANES : (t + 1) * LANES]
        return total

    def join(left, right):
        low = lax.broadcasted_iota(jnp.int32, (8, LANES), 1) < LANES // 2
        halves = [x + pltpu.roll(x, LANES // 2, 1) for x in (left, right)]
        return jnp.sum(jnp.where(low, *halves), axis=0, keepdims=True)

    if s is None:
        zero = jnp.zeros((8, LANES), jnp.float32)
        return join(fold(r * r), zero), join(fold(w * r), zero)
    return join(fold(r * r), fold(r * s + p * w)), join(fold(w * r), fold(p * s))


def full_sums(received, first):
    low = lax.broadcasted_iota(jnp.int32, (1, LANES), 1) < LANES // 2
    found = []
    for row in (first, first + 1):
        total = jnp.sum(received[:, row, :], axis=0, keepdims=True)
        for half in (jnp.where(low, total, 0.0), jnp.where(low, 0.0, total)):
            found.append(jnp.sum(half, axis=1, keepdims=True))
    return found[0], found[2], found[1], found[3]


def one_row(sums):
    upper, lower = sums
    quarter = LANES // 4
    lane = lax.broadcasted_iota(jnp.int32, (8, LANES), 1)
    upper, lower = [jnp.broadcast_to(x, (8, LANES)) for x in (upper, lower)]
    upper = upper + pltpu.roll(upper, quarter, 1)
    lower = lower + pltpu.roll(lower, LANES - quarter, 1)
    return jnp.where(jnp.bitwise_and(lane, quarter) != 0, upper, lower)[0:1, :]


def row_sums(received):
    total = jnp.sum(received[:, 0, :], axis=0, keepdims=True)
    part = lax.broadcasted_iota(jnp.int32, (1, LANES), 1) // (LANES // 4)
    return [
        jnp.sum(jnp.where(part == q, total, 0.0), axis=1, keepdims=True) for q in (1, 0, 3, 2)
    ]


def step_sizes(sums, past):
    gamma, delta, mixed, energy = sums
    beta = gamma / past[0:1, 0:1]
    return gamma / (delta + beta * (mixed + beta * energy)), beta


def far_tables(
    plan, stiff, received, mine, field, table, index, away, hot, local, merged,
):
    lane8 = lax.broadcasted_iota(jnp.int32, (8, LANES), 1)
    where = plan.neighbours()
    rows = plan.far
    for e in range(rows):
        own = pltpu.roll(mine[e * 8 : e * 8 + 8, :], plan.half, 1)
        packed = jnp.concatenate([received[where[e], 0], received[where[e], 1]], axis=0)
        chunk = jnp.concatenate([packed, pltpu.roll(packed, plan.half, 1)], axis=0)
        merged[e * 8 : e * 8 + 8, :] = jnp.where(lane8 < plan.half, chunk, own)
    mirror = lax.broadcasted_iota(jnp.int32, (rows, LANES), 1) < plan.half
    row = [row_of(merged, r, 8, rows) for r in range(8)]
    for c in range(3):
        table[c, 0:rows, :] = jnp.where(mirror, -row[3 + c], row[3 + c])
    table[3, 0:rows, :] = jnp.where(mirror, row[7], row[6])
    table[4, 0:rows, :] = jnp.where(mirror, row[6], row[7])
    for k, value in enumerate(coefficients(stiff, row[2], plan.types)):
        table[5 + k, 0:rows, :] = value
    here = jnp.where(mirror, row[1], row[0])
    index[0:rows, :] = here.astype(jnp.int32)
    away[0:rows, :] = jnp.where(mirror, row[0], row[1]).astype(jnp.int32)
    make = one_hot(here, plan.rim)
    tiles = [field[:, t * LANES : (t + 1) * LANES] for t in range(plan.rim_tiles)]
    for e in range(rows):
        hot[e * LANES : (e + 1) * LANES, :] = make(e)
        local[e * 8 : e * 8 + 8, :] = lane_gather(tiles, spread(index, e))


def far_first(
    plan, received, swapped, table, index, away, hot, local, field, image,
    w, message, local_new, there, push, left,
):
    where = plan.neighbours()
    half = lax.rem(lax.axis_index(AXES[2]), 2)
    for e in range(plan.far):
        wanted = spread(away, e)
        low = jnp.bitwise_and(wanted, LANES - 1)
        found = []
        for source in (received, swapped):
            rows = [source[where[e], 2 + i] for i in (0, 1, 2, 2)]
            tile = jnp.concatenate(rows, axis=0)
            found.append(jnp.take_along_axis(tile, low, axis=1, mode="promise_in_bounds"))
        there[e * 8 : e * 8 + 8, :] = jnp.where(
            lax.shift_right_logical(wanted, 7) == half, found[0], found[1]
        )
    queue = Queue()
    found = far_push(plan, local, there, table, hot, push, left, queue)
    queue.run()
    force = far_total(found)
    w[...] = image[...]
    w[:, 0 : plan.rim] = image[:, 0 : plan.rim] - force
    sums = partial_sums(field[...], w[...])
    send_rim(plan, w, index, sums, message, local_new)


def far_step(plan, number, *refs):
    refs = list(refs)

    def take(count):
        return [refs.pop(0) for _ in range(count)]

    received, diag, own, slot, near_const, near_hot, table, index, hot, local, r, w = take(12)
    if number:
        p, s, z, x, past = take(5)
    last = number == ITERS - 2
    r_new, p_new, s_new, x_new, w_new, past_new = take(6)
    if not last:
        z_new, message, local_new = take(3)
    else:
        (message,) = take(1)
    image, near_seen, near_push, near_left, there, push, left = take(7)

    where = plan.neighbours()
    for e in range(plan.far):
        there[e * 8 : e * 8 + 8, :] = received[where[e], :, :]
    sums = full_sums(received, FIELDS)
    queue = Queue()
    kept = []
    near_part(
        plan, w, diag, own, slot, near_const, near_hot, image, near_seen, near_push, near_left, queue,
        lambda: kept.append(far_push(plan, local, there, table, hot, push, left, queue)),
    )
    (found,) = kept
    force = far_total(found)
    q = jnp.concatenate(
        [image[:, 0 : plan.rim] - force, image[:, plan.rim :]], axis=1
    )
    if number:
        alpha, beta = step_sizes(sums, past)
        z_now = q + beta * z[...]
        s_now = w[...] + beta * s[...]
        p_now = r[...] + beta * p[...]
        x_new[...] = x[...] + alpha * p_now
    else:
        alpha = sums[0] / sums[1]
        z_now = q
        s_now = w[...]
        p_now = r[...]
        x_new[...] = alpha * p_now
    r_now = r[...] - alpha * s_now
    w_now = w[...] - alpha * z_now
    r_new[...] = r_now
    w_new[...] = w_now
    p_new[...] = p_now
    s_new[...] = s_now
    past_new[...] = jnp.broadcast_to(sums[0], past_new.shape)
    sums = partial_sums(r_now, w_now, s_now, p_now)
    if not last:
        z_new[...] = z_now
        send_rim(plan, w_new, index, sums, message, local_new)
    else:
        message[...] = jnp.broadcast_to(one_row(sums)[None], message.shape)


def finish(plan, received, r, w, p, s, x, past, x_out, r_out, x_last, r_last, sems):
    alpha, beta = step_sizes(row_sums(received), past)
    for t in range(plan.grain_tiles):
        here = slice(0, FIELDS), slice(t * LANES, (t + 1) * LANES)
        there = pl.ds(t, FIELDS, stride=plan.grain_tiles), slice(None)
        x_last[there] = x[here] + alpha * (r[here] + beta * p[here])
        r_last[there] = r[here] - alpha * (w[here] + beta * s[here])
    lines = pl.ds(0, FIELDS * plan.grain_tiles)
    for copy in fetch([(x_last.at[lines, :], x_out), (r_last.at[lines, :], r_out)], sems):
        copy.wait()


def shards(
    mesh,
    right_side,
    grain_diag,
    stiffness,
    contact_own,
    contact_slot,
    contact_type,
    contact_normal,
    contact_radii,
):
    plan = Plan(mesh, right_side.shape[-1], contact_own.shape[-1], stiffness.shape[1])
    own = contact_own.reshape(plan.tiles, LANES)
    slot = contact_slot.reshape(plan.tiles, LANES)
    kind = contact_type.reshape(plan.tiles, LANES)
    normal = contact_normal.reshape(3 * plan.tiles, LANES)
    lines = (FIELDS * plan.grain_tiles, LANES)
    more_lines = (8 * plan.grain_tiles, LANES)
    rhs = right_side.reshape(lines)
    ground = grain_diag.reshape(lines)
    f32, bf16, i32 = jnp.float32, jnp.bfloat16, jnp.int32
    vmem, hbm, dma = pltpu.MemorySpace.VMEM, pltpu.MemorySpace.HBM, pltpu.SemaphoreType.DMA
    wide = (8, plan.grains)
    far = (-(-plan.far // 8) * 64, LANES)
    far_table = (9, -(-plan.far // 8) * 8, LANES)
    near_table = (9, plan.tiles, LANES)
    table = (plan.tiles, LANES)
    near_rows = 2 * plan.near_tiles
    parts = plan.grains // plan.rim
    rest = plan.contacts - plan.near // LANES * LANES

    def call(body, outs, scratch, *args, raw=False, end=False):
        space = hbm if raw else vmem
        args = [pltpu.with_memory_space_constraint(x, space) for x in args]
        return pl.pallas_call(
            functools.partial(body, plan),
            out_shape=[(hbm if end else vmem)(dims, dtype) for dims, dtype in outs],
            in_specs=[pl.BlockSpec(memory_space=space)] * len(args),
            out_specs=[pl.BlockSpec(memory_space=hbm if end else vmem)] * len(outs),
            scratch_shapes=scratch,
            compiler_params=pltpu.CompilerParams(vmem_limit_bytes=16 * 2**20),
        )(*args)

    def exchange(message):
        return lax.all_to_all(message, AXES, 0, 0)

    tile = (plan.devices, 8, LANES)
    near_scratch = [
        vmem((near_rows * 8 + 64, LANES), f32),
        vmem((near_rows * 8 + 64, LANES), f32),
        vmem((parts * 24, near_rows * LANES), bf16),
    ]
    far_scratch = [vmem(far, f32), vmem(far, f32), vmem((32, plan.far * LANES), bf16)]

    message, mine = call(
        send_setup,
        [((plan.devices, 2 + FIELDS // 2, 2, LANES), f32), (far, f32)],
        [
            vmem(table, i32),
            vmem(table, i32),
            vmem(table, i32),
            vmem((8 * plan.tiles, LANES), f32),
            vmem((2, rest), f32),
            vmem(more_lines, f32),
            vmem((rest // LANES * 8, LANES), f32),
            dma((6,)),
        ],
        own, slot, kind, normal, contact_radii, rhs,
        raw=True,
    )
    received = exchange(message)
    image, near_const, field, diag, own, slot, stiff, near_hot = call(
        near_first,
        [
            (wide, f32),
            (near_table, f32),
            (wide, f32),
            (wide, f32),
            (table, i32),
            (table, i32),
            (stiffness.shape, f32),
            ((near_rows * LANES, plan.rim), bf16),
        ],
        [vmem(table, i32), vmem((2, plan.contacts), f32), vmem(more_lines, f32), vmem(more_lines, f32)]
        + near_scratch
        + [dma((10,))],
        stiffness, own, slot, kind, normal, contact_radii, rhs, ground,
        raw=True,
    )
    pairs = [(i, i ^ 1) for i in range(plan.counts[2])]
    received, image = lax.optimization_barrier((received, image))
    swapped = lax.ppermute(received, AXES[2], pairs)
    far_const, index, away, far_hot, local = call(
        far_tables,
        [
            (far_table, f32),
            (far_table[1:], i32),
            (far_table[1:], i32),
            ((plan.far * LANES, plan.rim), bf16),
            (far, f32),
        ],
        [vmem(far, f32)],
        stiff, received, mine, field,
    )
    w, message, local = call(
        far_first,
        [(wide, f32), (tile, f32), (far, f32)],
        far_scratch,
        received, swapped, far_const, index, away, far_hot, local, field, image,
    )
    r = field
    state = ()
    for number in range(ITERS - 1):
        received = exchange(message)
        last = number == ITERS - 2
        outs = [(wide, f32)] * 5 + [((8, LANES), f32)]
        if last:
            outs = outs + [((plan.devices, 1, LANES), f32)]
        else:
            outs = outs + [(wide, f32), (tile, f32), (far, f32)]
        made = call(
            lambda plan, *refs, number=number: far_step(plan, number, *refs),
            outs,
            [vmem(wide, f32)] + near_scratch + far_scratch,
            received, diag, own, slot, near_const, near_hot, far_const, index, far_hot, local, r, w, *state,
        )
        r, p, s, x, w, past = made[:6]
        if last:
            message = made[6]
        else:
            z, message, local = made[6:]
            state = (p, s, z, x, past)
    received = exchange(message)
    solution_field, residual = call(
        finish,
        [(lines, f32)] * 2,
        [vmem(more_lines, f32), vmem(more_lines, f32), dma((2,))],
        received, r, w, p, s, x, past,
        end=True,
    )
    return (solution_field.reshape(right_side.shape), residual.reshape(right_side.shape))


def solution(mesh):
    vector = P("gx", "gy", "gz", None)
    matrix = P("gx", "gy", "gz", None, None)
    return jax.shard_map(
        functools.partial(shards, mesh),
        mesh=mesh,
        in_specs=(matrix, matrix, P(), vector, vector, vector, matrix, matrix),
        out_specs=(matrix, matrix),
        check_vma=False,
    )
```
